32 devices in a mesh: dp: 16 (over z, y, core), tensor: 2 (over x).
Axes of the slice: x: 2, y: 2, z: 4, core: 2. Of those that a mesh axis runs over, the one named last changes fastest.
Arguments:
- layer_input: float32 [25216, 512], P('dp'), may hold values from -6 to 6
- cotangent: float32 [25216, 512], P('dp'), may hold values from -6 to 6
- ln1_gain: float32 [512], replicated, may hold values from 0.1 to 1.9
- ln1_shift: float32 [512], replicated, may hold values from -1.75 to 1.75
- w_qkv: bfloat16 [3, 512, 512], P(None, None, 'tensor'), may hold values from -0.375 to 0.375
- qv_bias: float32 [2, 512], P(None, 'tensor'), may hold values from -3 to 3
- w_out: bfloat16 [512, 512], P('tensor'), may hold values from -0.75 to 0.75
- out_bias: float32 [512], replicated, may hold values from -1.75 to 1.75
- ln2_gain: float32 [512], replicated, may hold values from 0.1 to 1.9
- ln2_shift: float32 [512], replicated, may hold values from -1.75 to 1.75
- w_router: float32 [512, 4], replicated, may hold values from -0.125 to 0.125
- w_in: bfloat16 [4, 512, 2048], P(None, None, 'tensor'), may hold values from -0.25 to 0.25
- in_bias: float32 [4, 2048], P(None, 'tensor'), may hold values from -1.75 to 1.75
- w_hidden_out: bfloat16 [4, 2048, 512], P(None, 'tensor'), may hold values from -0.5 to 0.5
- choices: int32 [25216, 2], P('dp'), may hold values from 0 to 3, as said below
- priority: int32 [16, 1576], P('dp'), may hold values from 0 to 1575, each once within a row
Outputs:
- layer_out: float32 [25216, 512], P('dp')
- input_grad: float32 [25216, 512], P('dp')
- ln1_gain_grad: float32 [512], replicated
- ln1_shift_grad: float32 [512], replicated
- w_qkv_grad: float32 [3, 512, 512], P(None, None, 'tensor')
- qv_bias_grad: float32 [2, 512], P(None, 'tensor')
- w_out_grad: float32 [512, 512], P('tensor')
- out_bias_grad: float32 [512], replicated
- ln2_gain_grad: float32 [512], replicated
- ln2_shift_grad: float32 [512], replicated
- w_router_grad: float32 [512, 4], replicated
- w_in_grad: float32 [4, 512, 2048], P(None, None, 'tensor')
- in_bias_grad: float32 [4, 2048], P(None, 'tensor')
- w_hidden_out_grad: float32 [4, 2048, 512], P(None, 'tensor')
The draws below stay inside these ranges and needn't reach their ends.
Inputs may be any that keep to these rules, and one draw needn't show every extreme that they name: `choices`: each row names two different experts; every expert is named by some row. `priority`: each row is a permutation of 0 to 1575 giving the dispatch rank of the tokens of one data shard, lower first.
All inputs are finite; a program needn't handle non-finite values.
Results may differ from the reference program's by a relative error of at most 0.013.
The reference program's roundings to bfloat16 on the way count: a program that leaves them out, or rounds other values in their place, can miss the bound.
Values sent between devices are 32-bit elements; how exact they have to be, the bound alone decides.
A program may use at most 192 MiB of HBM per device.

```python
import jax
import jax.numpy as jnp
from jax import lax

D = 512
HEADS = 8
HEAD_DIM = 64
FF = 2048
EXPERT_TOTAL = 4
SEQ = 197
TOK_DEV = 1576
CAPACITY = 985
TOKENS = 25216
N_DP = 16


def draw_choices(key, part):
    key = jax.random.fold_in(key, 11)
    favour_key, score_key = jax.random.split(key)
    favoured = jax.random.randint(favour_key, (N_DP,), 0, EXPERT_TOTAL)
    token_ids = jnp.arange(TOKENS, dtype=jnp.int32)
    expert_index_list = jnp.arange(EXPERT_TOTAL, dtype=jnp.int32)
    shard_preferred_expert = favoured[token_ids // TOK_DEV]
    starting_scores = jax.random.randint(score_key, (TOKENS, EXPERT_TOTAL), 0, 1000)
    favour_boost = jnp.where(shard_preferred_expert[:, None] == expert_index_list[None, :], 400, 0)
    forced_choice = jnp.where((token_ids[:, None] < EXPERT_TOTAL) & (token_ids[:, None] == expert_index_list[None, :]), 5000, 0)
    grand_total = (starting_scores + favour_boost + forced_choice) * EXPERT_TOTAL + expert_index_list[None, :]
    top_vals, top_ids = lax.top_k(grand_total, 2)
    return top_ids.astype(jnp.int32)


def steps_of(key, extent, pieces, least, high):
    gain = 1.0
    for dim, blocks in pieces:
        heights = jax.random.uniform(jax.random.fold_in(jax.random.fold_in(key, 6), dim), (blocks,), jnp.float32, least / len(pieces), high / len(pieces))
        gain = gain * jnp.repeat(jnp.exp(heights), extent[dim] // blocks).reshape((-1,) + (1,) * (len(extent) - 1 - dim))
    return gain


def noise(key, extent, width, limit, shards=(), kind=jnp.bfloat16):
    gain = steps_of(key, extent, shards, -0.22, 0.18) if shards else 1.0
    values = jax.random.normal(key, extent, jnp.float32) * width * gain
    return jnp.minimum(jnp.maximum(values, -limit), limit).astype(kind)


def setup_inputs(seed: int = 0) -> dict:
    key_list = jax.random.split(jax.random.key(seed), 17)
    layer_input = noise(key_list[0], (TOKENS, D), 1.0, 6.0, ((0, 16),), jnp.float32)
    cotangent = noise(key_list[1], (TOKENS, D), 1.0, 6.0, ((0, 16),), jnp.float32)
    ln1_gain = jnp.clip(1.0 + 0.18 * jax.random.normal(key_list[2], (D,), jnp.float32), 0.1, 1.9)
    ln1_shift = noise(key_list[3], (D,), 0.3, 1.75, (), jnp.float32)
    w_qkv = noise(key_list[4], (3, D, D), (D // 2) ** -0.5, 0.375, ((2, 2),))
    qv_bias = noise(key_list[5], (2, D), 0.5, 3.0, ((1, 2),), jnp.float32)
    w_out = noise(key_list[6], (D, D), (D // 8) ** -0.5, 0.75, ((0, 2),))
    out_bias = noise(key_list[7], (D,), 0.3, 1.75, (), jnp.float32)
    ln2_gain = jnp.clip(1.0 + 0.18 * jax.random.normal(key_list[8], (D,), jnp.float32), 0.1, 1.9)
    ln2_shift = noise(key_list[9], (D,), 0.3, 1.75, (), jnp.float32)
    w_router = noise(key_list[10], (D, EXPERT_TOTAL), (4 * D) ** -0.5, 0.125, (), jnp.float32)
    w_in = noise(key_list[11], (EXPERT_TOTAL, D, FF), D ** -0.5, 0.25, ((2, 2),))
    in_bias = noise(key_list[12], (EXPERT_TOTAL, FF), 0.3, 1.75, ((1, 2),), jnp.float32)
    w_hidden_out = noise(key_list[13], (EXPERT_TOTAL, FF, D), (FF // 16) ** -0.5, 0.5, ((1, 2),))
    choices = draw_choices(jax.random.fold_in(key_list[16], 71), 0)
    priority = jax.vmap(lambda own: jax.random.permutation(own, TOK_DEV))(jax.random.split(key_list[15], N_DP)).reshape((N_DP, TOK_DEV)).astype(jnp.int32)
    return dict(layer_input=layer_input, cotangent=cotangent, ln1_gain=ln1_gain, ln1_shift=ln1_shift, w_qkv=w_qkv, qv_bias=qv_bias, w_out=w_out, out_bias=out_bias, ln2_gain=ln2_gain, ln2_shift=ln2_shift, w_router=w_router, w_in=w_in, in_bias=in_bias, w_hidden_out=w_hidden_out, choices=choices, priority=priority)


@jax.custom_vjp
def low(v):
    return lax.optimization_barrier(v.astype(jnp.bfloat16)).astype(jnp.float32)

@jax.custom_vjp
def low_back(v):
    return v

def low_keep(v):
    return (low(v), None)

def low_pass(kept, grad):
    return (grad,)

def back_keep(v):
    return (v, None)

def back_low(kept, grad):
    return (low(grad),)
low.defvjp(low_keep, low_pass)
low_back.defvjp(back_keep, back_low)
epsilon = 1e-06
HIGHEST = lax.Precision.HIGHEST

def layer_norm(inputs, ln_gain, ln_shift):
    row_mean = lax.optimization_barrier(jnp.mean(inputs, axis=-1, keepdims=True))
    centred = inputs - row_mean
    row_var = lax.optimization_barrier(jnp.mean(centred * centred, axis=-1, keepdims=True))
    return centred * lax.rsqrt(row_var + epsilon) * ln_gain + ln_shift

def softmax_rows(scores):
    row_max = lax.optimization_barrier(jnp.max(scores, axis=-1, keepdims=True))
    exp_rows = jnp.exp(scores - row_max)
    return exp_rows / lax.optimization_barrier(jnp.sum(exp_rows, axis=-1, keepdims=True))

def slot_table(choices, priority, experts_n, capacity):
    tok_count = choices.shape[0]
    token_ids = jnp.arange(tok_count, dtype=jnp.int32)
    ranked_ids = jnp.zeros((tok_count,), jnp.int32).at[priority].set(token_ids)
    ranked_choice = choices[ranked_ids]
    onehot = (ranked_choice.T[:, :, None] == jnp.arange(experts_n, dtype=jnp.int32)[None, None, :]).astype(jnp.int32)
    flat_hits = onehot.reshape(2 * tok_count, experts_n)
    earlier = jnp.cumsum(flat_hits, axis=0) - flat_hits
    position = lax.optimization_barrier(jnp.sum(earlier * flat_hits, axis=1)).reshape(2, tok_count)
    position = position[:, priority].T
    kept_mask = position < capacity
    slot_ids = jnp.where(kept_mask, choices * capacity + position, experts_n * capacity).astype(jnp.int32)
    pair_token = jnp.broadcast_to(token_ids[:, None], (tok_count, 2))
    slot_token = jnp.full((experts_n * capacity + 1,), tok_count, jnp.int32).at[slot_ids.reshape(-1)].set(pair_token.reshape(-1))
    return (slot_ids, kept_mask, slot_token[:experts_n * capacity])

def forward(params, inputs, choices, slot_ids, kept_mask, slot_token):
    ln1_gain, ln1_shift, w_qkv, qv_bias, w_out, out_bias, ln2_gain, ln2_shift, w_router, w_in, in_bias, w_hidden_out = params
    tok_count = inputs.shape[0]
    head_shape = (tok_count // SEQ, SEQ, HEADS, HEAD_DIM)
    normed = low(layer_norm(inputs, ln1_gain, ln1_shift))
    projected = jnp.einsum('td,jdf->jtf', normed, w_qkv, precision=HIGHEST)
    queries = low(low_back(projected[0] + qv_bias[0])).reshape(head_shape)
    key_rows = low(low_back(projected[1])).reshape(head_shape)
    value_rows = low(low_back(projected[2] + qv_bias[1])).reshape(head_shape)
    scores = low_back(jnp.einsum('bqhd,bkhd->bhqk', queries, key_rows, precision=HIGHEST) * HEAD_DIM ** (-0.5))
    softmaxed = low(softmax_rows(scores))
    attended = jnp.einsum('bhqk,bkhd->bqhd', softmaxed, value_rows, precision=HIGHEST).reshape(tok_count, D)
    attended = low(low_back(attended))
    branch = low_back(jnp.dot(attended, w_out, precision=HIGHEST) + out_bias)
    middle = inputs + branch
    routed_in = low(layer_norm(middle, ln2_gain, ln2_shift))
    router = softmax_rows(jnp.dot(routed_in, w_router, precision=HIGHEST))
    gates = jnp.take_along_axis(router, choices, axis=1)
    padded = jnp.concatenate([routed_in, jnp.zeros((1, D), jnp.float32)], axis=0)
    expert_in = padded[slot_token].reshape(EXPERT_TOTAL, CAPACITY, D)
    pre_act = low_back(jnp.einsum('ecd,edf->ecf', expert_in, w_in, precision=HIGHEST) + in_bias[:, None, :])
    hidden = low(jax.nn.gelu(pre_act, approximate=True))
    expert_out = low_back(jnp.einsum('ecf,efd->ecd', hidden, w_hidden_out, precision=HIGHEST))
    out_pad = jnp.concatenate([expert_out.reshape(EXPERT_TOTAL * CAPACITY, D), jnp.zeros((1, D), jnp.float32)], axis=0)
    pair_weight = jnp.where(kept_mask, low(gates), jnp.float32(0.0))
    combined = pair_weight[:, 0:1] * out_pad[slot_ids[:, 0]] + pair_weight[:, 1:2] * out_pad[slot_ids[:, 1]]
    return middle + combined

def reference(layer_input, cotangent, ln1_gain, ln1_shift, w_qkv, qv_bias, w_out, out_bias, ln2_gain, ln2_shift, w_router, w_in, in_bias, w_hidden_out, choices, priority):
    params = tuple((item.astype(jnp.float32) for item in (ln1_gain, ln1_shift, w_qkv, qv_bias, w_out, out_bias, ln2_gain, ln2_shift, w_router, w_in, in_bias, w_hidden_out)))
    shard_input = layer_input.astype(jnp.float32).reshape(N_DP, TOK_DEV, D)
    shard_cot = cotangent.astype(jnp.float32).reshape(N_DP, TOK_DEV, D)
    shard_choice = choices.reshape(N_DP, TOK_DEV, 2)

    def shard_step(summed, shard_item):
        inputs, cot_rows, choice_rows, priority_row = shard_item
        slot_ids, kept_mask, slot_token = slot_table(choice_rows, priority_row, EXPERT_TOTAL, CAPACITY)

        def forward_fn(weights, rows):
            return forward(weights, rows, choice_rows, slot_ids, kept_mask, slot_token)
        outputs, pullback = jax.vjp(jax.checkpoint(forward_fn), params, inputs)
        grad_params, grad_input = pullback(cot_rows)
        summed = jax.tree.map(lambda left, right: left + right, summed, grad_params)
        return (summed, (outputs, grad_input))
    initial = jax.tree.map(jnp.zeros_like, params)
    summed, (outputs, grad_input) = lax.scan(shard_step, initial, (shard_input, shard_cot, shard_choice, priority))
    return (outputs.reshape(N_DP * TOK_DEV, D), grad_input.reshape(N_DP * TOK_DEV, D), summed[0], summed[1], summed[2], summed[3], summed[4], summed[5], summed[6], summed[7], summed[8], summed[9], summed[10], summed[11])
```

```python
import functools

import jax
import jax.numpy as jnp
from jax import lax
from jax.experimental import pallas as pl
from jax.experimental.pallas import tpu as pltpu
from jax.sharding import PartitionSpec as P

HEAD_DIM = 64
SEQ = 197
PAD = 208
SENT = 200
LANES = 128
EPS = 1e-06
SCALE = HEAD_DIM ** (-0.5)
BF = jnp.bfloat16
F32 = jnp.float32
MESH = pl.DeviceIdType.MESH
MIB = 1 << 20

UNITS = 18
ENTRIES = 20
SLOTS = 4
FINALS = 8
FIRST_ATT = 16
SMALL = 24


def dot(a, b):
    return jnp.dot(a, b, preferred_element_type=F32)


def dot_nt(a, b):
    return lax.dot_general(a, b, (((1,), (1,)), ((), ())), preferred_element_type=F32)


def dot_tn(a, b):
    return lax.dot_general(a, b, (((0,), (0,)), ((), ())), preferred_element_type=F32)


def rows(i, size):
    return pl.ds(pl.multiple_of(i * size, size), size)


def span(start, size):
    return pl.ds(pl.multiple_of(start, 32), size)


def iota(shape, axis):
    return lax.broadcasted_iota(jnp.int32, shape, axis)


def column(vals, index):
    return jnp.sum(jnp.where(iota(vals.shape, 1) == index, vals, 0.0), axis=1, keepdims=True)


def norm_stats(vals):
    centred = vals - jnp.mean(vals, axis=1, keepdims=True)
    inv = lax.rsqrt(jnp.mean(centred * centred, axis=1, keepdims=True) + EPS)
    return centred * inv, inv


def norm_back(grad, gain, unit, inv):
    scaled = grad * gain
    mean_one = jnp.mean(scaled, axis=1, keepdims=True)
    mean_two = jnp.mean(scaled * unit, axis=1, keepdims=True)
    return inv * (scaled - mean_one - unit * mean_two)


def split_three(vals):
    high = vals.astype(BF)
    rest = vals - high.astype(F32)
    mid = rest.astype(BF)
    low = (rest - mid.astype(F32)).astype(BF)
    return high, mid, low


def spread(flat_ref, padded_ref, images):
    for i in range(images):
        padded_ref[pl.ds(i * PAD + PAD - 16, 16), :] = jnp.zeros((16, padded_ref.shape[1]), F32)
        padded_ref[pl.ds(i * PAD, SEQ), :] = flat_ref[pl.ds(i * SEQ, SEQ), :]


def close_up(ref, images):
    for i in range(1, images):
        ref[pl.ds(i * SEQ, SEQ), :] = ref[pl.ds(i * PAD, SEQ), :]


def two_heads(pair):
    low = iota(pair.shape, 1) < HEAD_DIM
    zero = jnp.zeros_like(pair)
    gap = jnp.zeros((256 - PAD, LANES), pair.dtype)
    return jnp.concatenate([jnp.where(low, pair, zero), gap, jnp.where(low, zero, pair), gap], axis=0)


def one_pair(wide):
    merged = jnp.where(iota((LANES, 256), 0) < HEAD_DIM, wide[:, 0:256], wide[:, 256:512])
    return jnp.transpose(merged)[0:PAD]


def pair_probs(keys, q_wide):
    scores = dot_nt(keys, q_wide)
    tail = scores[PAD - 16 :]
    tail = jnp.where(iota(tail.shape, 0) < SEQ - (PAD - 16), tail, -1e30)
    scores = jnp.concatenate([scores[: PAD - 16], tail], axis=0)
    exps = jnp.exp(scores - jnp.max(scores, axis=0, keepdims=True))
    return exps * (1.0 / jnp.sum(exps, axis=0, keepdims=True))


def main_kernel(
    n_dp,
    images,
    capacity,
    x_hbm,
    cot_hbm,
    choice_ref,
    prio_ref,
    g1_ref,
    b1_ref,
    wqkv_ref,
    qvb_ref,
    wo_ref,
    ob_ref,
    g2_ref,
    b2_ref,
    wr_ref,
    win_hbm,
    ib_ref,
    wout_hbm,
    out_hbm,
    layer_hbm,
    grad_hbm,
    smallsum_ref,
    rgl_hbm,
    combl_hbm,
    qkv_hbm,
    normed_hbm,
    att_hbm,
    mid_hbm,
    xp_hbm,
    smalls_hbm,
    xs_ref,
    gp_ref,
    wts_ref,
    win_ref,
    wout_ref,
    og_ref,
    h_ref,
    dg_ref,
    comb_ref,
    rg_ref,
    gate_ref,
    acc_ref,
    sib_ref,
    landc_ref,
    landy_ref,
    landr_ref,
    landl_ref,
    fin_ref,
    gt_ref,
    gtl_ref,
    small_ref,
    sm_ref,
    dwr_ref,
    wqo_ref,
    woo_ref,
    bias_ref,
    qkvb_ref,
    bufa_ref,
    bufb_ref,
    bufc_ref,
    load_sem,
    save_sem,
    fx_sem,
    fy_sem,
    fs_sem,
    fb_sem,
    qkv_sem,
    img_sem,
    rgs_sem,
    rgr_sem,
    cs_sem,
    cr_sem,
    gt_sem,
    sib_sem,
    landc_sem,
    ys_sem,
    yr_sem,
    rs_sem,
    rr_sem,
    ls_sem,
    lr_sem,
    brs_sem,
    brr_sem,
    bls_sem,
    blr_sem,
    ars_sem,
    arr_sem,
    als_sem,
    alr_sem,
    ks_sem,
    kr_sem,
    kl_sem,
    loc_sem,
    sms_sem,
    smr_sem,
    credit_r,
    credit_l,
):
    total = images * PAD
    flat = images * SEQ
    tiles = total // 416
    nz = n_dp // 4
    deep = nz > 4
    held = acc_ref.shape[0]
    dp = lax.axis_index("dp")
    tensor = lax.axis_index("tensor")
    core = lax.rem(dp, 2)
    y = lax.rem(lax.div(dp, 2), 2)
    z = lax.div(dp, 4)
    across = {"tensor": 1 - tensor}
    sibling = {"dp": dp + 1 - 2 * core}
    ypal = {"dp": dp + 2 - 4 * y}
    right = {"dp": lax.rem(dp + 4, n_dp)}
    left = {"dp": lax.rem(dp + n_dp - 4, n_dp)}
    first, last = z == 0, z == nz - 1

    def remote(src, dst, send, recv, where):
        return pltpu.make_async_remote_copy(src, dst, send, recv, where, MESH)

    def local_copy(src, dst, sem):
        return pltpu.make_async_copy(src, dst, sem)

    flat_rows = pl.ds(0, flat)
    x_load = local_copy(x_hbm, comb_ref.at[flat_rows, :], load_sem.at[8])
    x_load.start()
    weight_loads = []
    for e in range(4):
        weight_loads.append(local_copy(win_hbm.at[e], win_ref.at[e], load_sem.at[e]))
        weight_loads.append(local_copy(wout_hbm.at[e], wout_ref.at[e], load_sem.at[4 + e]))
    barrier = pltpu.get_barrier_semaphore()
    pl.semaphore_signal(barrier, inc=1, device_id=across, device_id_type=MESH)

    @pl.loop(1, n_dp)
    def _(d):
        pl.semaphore_signal(
            barrier, inc=1, device_id={"dp": lax.rem(dp + d, n_dp)}, device_id_type=MESH
        )

    def land(j, half):
        return acc_ref.at[j, :, rows(half, 256)]

    half_rows = rows(core, 256)

    @pl.when(y == 0)
    def _():
        acc_ref[4, :, 0:256] = wqkv_ref[0, half_rows, :].astype(F32)
        acc_ref[5, :, 0:256] = wqkv_ref[2, half_rows, :].astype(F32)

    @pl.when(y == 1)
    def _():
        acc_ref[4, :, 0:256] = wqkv_ref[1, half_rows, :].astype(F32)
        acc_ref[5, :, 0:256] = wo_ref[:, half_rows].astype(F32)

    pl.semaphore_wait(barrier, n_dp)

    def fetch_x(t):
        src = acc_ref.at[4 + t, :, pl.ds(0, 256)]
        return remote(src, land(y + 2 * t, core), fx_sem.at[0, t], fx_sem.at[1, t], across)

    def fetch_y(t, mine):
        j = (y if mine else 1 - y) + 2 * t
        return remote(land(j, core), land(j, core), fy_sem.at[0, t], fy_sem.at[1, t], ypal)

    def fetch_sib(j, half):
        return remote(land(j, half), land(j, half), fs_sem.at[0, j], fs_sem.at[1, j], sibling)

    for t in range(2):
        fetch_x(t).start()
    fetch_bias = remote(qvb_ref, bias_ref, fb_sem.at[0], fb_sem.at[1], across)
    fetch_bias.start()
    for copy in weight_loads:
        copy.start()

    x_load.wait()
    spread(comb_ref, rg_ref, images)
    cot_load = local_copy(cot_hbm, comb_ref.at[flat_rows, :], load_sem.at[8])
    cot_load.start()
    xp_save = local_copy(rg_ref, xp_hbm, save_sem.at[0])
    xp_save.start()
    n_cols = pl.ds(512, 512)

    @pl.loop(0, images)
    def _(i):
        r = rows(i, PAD)
        unit, _ = norm_stats(rg_ref[r, :])
        dg_ref[3, r, n_cols] = (unit * g1_ref[...] + b1_ref[...]).astype(BF)

    normed_save = local_copy(dg_ref.at[3, :, n_cols], normed_hbm, save_sem.at[1])
    normed_save.start()

    def qkv_view(j, side):
        return (0, 0, 1)[j], (0, 512, 0)[j] + side * 256

    def project(side, weights, biases):
        @pl.loop(0, tiles)
        def _(m):
            r = rows(m, 416)
            for j in range(3):
                out = dot(dg_ref[3, r, n_cols], weights[j])
                if j == 0:
                    out = (out + biases[0:1, :]) * SCALE
                if j == 2:
                    out = out + biases[1:2, :]
                a, c = qkv_view(j, side)
                dg_ref[a, r, pl.ds(c, 256)] = out.astype(BF)

    def attend(side, start, stop):
        @pl.loop(start, stop)
        def _(i):
            r = rows(i, PAD)
            for p in range(2):
                c = side * 256 + p * LANES
                probs = pair_probs(
                    dg_ref[0, r, pl.ds(512 + c, LANES)], two_heads(dg_ref[0, r, pl.ds(c, LANES)])
                )
                wide = dot_tn(dg_ref[1, r, pl.ds(c, LANES)], probs.astype(BF))
                h_ref[r, pl.ds(c, LANES)] = one_pair(wide).astype(BF)

    project(0, wqkv_ref, qvb_ref)
    attend(0, 0, images // 2)
    for t in range(2):
        fetch_x(t).wait_recv()
        fetch_y(t, True).start()
        fetch_sib(y + 2 * t, core).start()
    attend(0, images // 2, images)
    for t in range(2):
        fetch_y(t, False).wait_recv()
        fetch_sib(1 - y + 2 * t, core).start()

    gt_ref[...] = jnp.full(gt_ref.shape, 1e6, F32)
    gt_ref[0:2, 0:flat] = choice_ref[...].astype(F32)
    gt_ref[2:3, 0:flat] = prio_ref[...].astype(F32)
    gate_ref[:, 0:8] = jnp.transpose(gt_ref[...])
    lane = iota((total, LANES), 1).astype(F32)
    hot0 = (gate_ref[:, 0:1] == lane).astype(F32)
    og_ref[:, 0:128] = hot0.astype(BF)
    og_ref[:, 128:256] = (gate_ref[:, 1:2] == lane).astype(F32).astype(BF)
    total0 = jnp.sum(hot0, axis=0, keepdims=True)

    @pl.loop(0, images)
    def _(i):
        own = gate_ref[pl.ds(i * SEQ, PAD), :]
        lane_r = iota((PAD, LANES), 1).astype(F32)
        earlier = (gt_ref[2:3, :] < own[:, 2:3]).astype(F32).astype(BF)
        pos = dot(earlier, og_ref[:, 0:256])
        kept0 = (own[:, 0:1] == lane_r) & (pos[:, 0:128] < capacity)
        kept1 = (own[:, 1:2] == lane_r) & (pos[:, 128:256] + total0 < capacity)
        real = iota((PAD, LANES), 0) < SEQ
        wts_ref[rows(i, PAD), :] = jnp.where((kept0 | kept1) & real, 1.0, 0.0)

    cot_load.wait()
    spread(comb_ref, gp_ref, images)

    wr_wide = jnp.transpose(
        jnp.concatenate([wr_ref[...], jnp.zeros((LANES - 4, wr_ref.shape[1]), F32)], axis=0)
    )
    wr_parts = split_three(wr_wide)

    fetch_bias.wait_recv()
    for j in range(4):
        fetch_sib(j, 1 - core).wait_recv()
    for j in range(3):
        wqo_ref[j, 0:256, :] = acc_ref[j, :, 0:256].astype(BF)
        wqo_ref[j, 256:512, :] = acc_ref[j, :, 256:512].astype(BF)
    woo_ref[...] = acc_ref[3].astype(BF)
    project(1, wqo_ref, bias_ref)
    qkv_saves = []
    for j in range(3):
        a, c = qkv_view(j, 0)
        qkv_saves.append(local_copy(dg_ref.at[a, :, pl.ds(c, 512)], qkv_hbm.at[j], save_sem.at[2 + j]))
        qkv_saves[-1].start()
    attend(1, 0, images)
    att_save = local_copy(h_ref.at[:, pl.ds(0, 256)], att_hbm, save_sem.at[5])
    att_save.start()

    @pl.loop(0, tiles)
    def _(m):
        r = rows(m, 416)
        branch = dot(h_ref[r, 0:256], wo_ref[...]) + dot(h_ref[r, 256:512], woo_ref[...])
        middle = rg_ref[r, :] + (branch + ob_ref[...])
        comb_ref[r, :] = middle
        unit, _ = norm_stats(middle)
        routed = (unit * g2_ref[...] + b2_ref[...]).astype(BF)
        xs_ref[r, :] = routed
        logits = dot(routed, wr_parts[0]) + dot(routed, wr_parts[1]) + dot(routed, wr_parts[2])
        logits = jnp.where(iota(logits.shape, 1) < 4, logits, -1e30)
        exps = jnp.exp(logits - jnp.max(logits, axis=1, keepdims=True))
        router = exps / jnp.sum(exps, axis=1, keepdims=True)
        kept = wts_ref[r, :]
        wts_ref[r, :] = (
            kept * router.astype(BF).astype(F32) + pltpu.roll(router, 4, 1) + pltpu.roll(kept, 8, 1)
        )

    mid_save = local_copy(comb_ref, mid_hbm, save_sem.at[6])
    mid_save.start()
    gate_ref[...] = jnp.zeros_like(gate_ref)
    small_ref[...] = jnp.zeros_like(small_ref)
    dwr_ref[...] = jnp.zeros_like(dwr_ref)
    for copy in weight_loads:
        copy.wait()
    for t in range(2):
        fetch_x(t).wait_send()
        fetch_y(t, True).wait_send()
    for j in range(4):
        fetch_sib(j, core).wait_send()
    fetch_bias.wait_send()
    for copy in [xp_save, normed_save, att_save, mid_save] + qkv_saves:
        copy.wait()
    comb_ref[...] = jnp.zeros_like(comb_ref)
    rg_ref[...] = jnp.zeros_like(rg_ref)

    def place(n, start, size):
        return out_hbm.at[n, span(core * 256 + start, size), :]

    def part(n, start, size):
        return acc_ref.at[lax.rem(n, held), span(start, size), :]

    def add(n, start, size, land_ref):
        acc_ref[lax.rem(n, held), span(start, size), :] += land_ref[...]

    def final(n, start, size):
        if deep:
            return place(n, start, size)
        return fin_ref.at[lax.rem(n, FINALS), span(start, size), :]

    def exchange_sib(n):
        slot = lax.rem(n, 2)
        return remote(
            sib_ref.at[slot], landc_ref.at[slot], sib_sem.at[slot], landc_sem.at[slot], sibling
        )

    def absorb(n):
        exchange_sib(n).wait_recv()
        acc_ref[lax.rem(n, held)] += landc_ref[lax.rem(n, 2)]

    ya = y * 128

    class Entry:
        def __init__(self, kind, v):
            self.kind = kind
            if kind == "C":
                self.there = (v >= FIRST_ATT) & (v < FIRST_ATT + 4)
                self.q = v - FIRST_ATT + 16
                self.n = 16 + lax.div(self.q - 16, 2)
                self.piece = lax.rem(self.q, 2)
                self.yrows = 64
                self.base = self.piece * 64
                self.turn = lax.rem(self.q, 2)
            else:
                self.there = (v >= 0) & (v < 16) & (lax.rem(v, 2) == (0 if kind == "A" else 1))
                self.q = v
                self.n = self.q
                self.yrows = 128
                self.base = 0
                self.turn = lax.rem(lax.div(self.q, 2), 2) + (2 if kind == "B" else 0)
            if kind == "B":
                self.right, self.left = (0, 128), (128, 128)
            else:
                size = self.yrows // 2
                self.right = (ya + self.base, size)
                self.left = (ya + self.base + size, size)

        def half(self, to_right):
            return self.right if to_right else self.left

        def y_copy(self, start):
            land_ref = landy_ref.at[self.turn, pl.ds(0, self.yrows), :]
            return remote(
                part(self.n, start, self.yrows), land_ref, ys_sem.at[self.q], yr_sem.at[self.q], ypal
            ), land_ref

        def chain_copy(self, to_right):
            start, size = self.half(to_right)
            land_ref = (landr_ref if to_right else landl_ref).at[
                lax.rem(self.q, SLOTS), pl.ds(0, size), :
            ]
            send, recv = (rs_sem, rr_sem) if to_right else (ls_sem, lr_sem)
            where = right if to_right else left
            return remote(
                part(self.n, start, size), land_ref, send.at[self.q], recv.at[self.q], where
            ), land_ref

        def spread_copy(self, src, of_right):
            send, recv = (brs_sem, brr_sem) if of_right else (bls_sem, blr_sem)
            return remote(
                src, self.spot(of_right), send.at[self.q], recv.at[self.q], left if of_right else right
            )

        def spot(self, of_right):
            return final(self.n, *self.half(of_right))

        def rows_of(self, of_right):
            return part(self.n, *self.half(of_right))

        def y_final(self, src, of_right):
            send, recv = (ars_sem, arr_sem) if of_right else (als_sem, alr_sem)
            return remote(src, self.spot(of_right), send.at[self.q], recv.at[self.q], ypal)

        def y_final_in(self, of_right):
            start, size = self.half(of_right)
            spot = final(self.n, start + 128 - 2 * ya, size)
            send, recv = (ars_sem, arr_sem) if of_right else (als_sem, alr_sem)
            return remote(spot, spot, send.at[self.q], recv.at[self.q], ypal)

        def keep(self, of_right):
            return local_copy(self.rows_of(of_right), self.spot(of_right), loc_sem.at[self.q])

    def core_final(n, half):
        return remote(
            final(n, 0, 256), out_hbm.at[n, rows(half, 256), :], ks_sem.at[n], kr_sem.at[n], sibling
        )

    def own_final(n):
        return local_copy(final(n, 0, 256), place(n, 0, 256), kl_sem.at[n])

    def at_entry(kind, v, cond, body):
        entry = Entry(kind, v)

        @pl.when(entry.there & cond)
        def _():
            body(entry)

    def finish(entry, of_right):
        src = entry.rows_of(of_right)
        if deep:
            entry.keep(of_right).start()
        else:
            start, size = entry.half(of_right)
            fin_ref[lax.rem(entry.n, FINALS), span(start, size), :] = src[...]
            src = entry.spot(of_right)
        entry.spread_copy(src, of_right).start()
        if entry.kind != "B":
            entry.y_final(src, of_right).start()

    def service(s, kinds="AB"):
        for of_right in (True, False):
            source = last if of_right else first
            sink = first if of_right else last
            v = s - nz - ((nz - 1 - z) if of_right else z)

            def passed_on(entry, of_right=of_right, sink=sink):
                here = entry.spot(of_right)
                entry.spread_copy(here, of_right).wait_recv()

                @pl.when(jnp.logical_not(sink))
                def _():
                    entry.spread_copy(here, of_right).start()

                if entry.kind != "B":
                    entry.y_final(here, of_right).start()

            for kind in kinds:
                at_entry(kind, v, jnp.logical_not(source), passed_on)

        def y_in(entry):
            copy, land_ref = entry.y_copy(128 - ya + entry.base)
            copy.wait_recv()
            add(entry.n, ya + entry.base, entry.yrows, land_ref)

        def y_out(entry):
            entry.y_copy(128 - ya + entry.base)[0].start()

        for kind in kinds:
            if kind != "B":
                at_entry(kind, s - 1, True, y_in)
        for kind in kinds:
            if kind != "B":
                at_entry(kind, s, True, y_out)

        for kind in kinds:
            for to_right in (True, False):
                hop = z if to_right else nz - 1 - z
                v = s - hop - (0 if kind == "B" else 1)
                head, end = (first, last) if to_right else (last, first)
                credit = credit_r if to_right else credit_l
                back = left if to_right else right

                def chain(entry, to_right=to_right, head=head, end=end, credit=credit, back=back):
                    copy, land_ref = entry.chain_copy(to_right)
                    start, size = entry.half(to_right)

                    @pl.when(jnp.logical_not(head))
                    def _():
                        copy.wait_recv()
                        add(entry.n, start, size, land_ref)

                        @pl.when(entry.q + SLOTS < ENTRIES)
                        def _():
                            pl.semaphore_signal(credit, inc=1, device_id=back, device_id_type=MESH)

                    @pl.when(jnp.logical_not(end))
                    def _():
                        @pl.when(entry.q >= SLOTS)
                        def _():
                            pl.semaphore_wait(credit, 1)

                        copy.start()

                    @pl.when(end)
                    def _():
                        if entry.kind == "B":
                            entry.y_copy(start)[0].start()
                        else:
                            finish(entry, to_right)

                at_entry(kind, v, True, chain)

        if "B" in kinds:
            for to_right in (True, False):

                def root(entry, to_right=to_right):
                    start, size = entry.half(to_right)
                    copy, land_ref = entry.y_copy(start)
                    copy.wait_send()
                    copy.wait_recv()
                    add(entry.n, start, size, land_ref)
                    finish(entry, to_right)

                at_entry("B", s - nz, last if to_right else first, root)

        def landed(entry):
            for of_right in (True, False):
                if entry.kind != "B":
                    entry.y_final_in(of_right).wait_recv()

                if deep:

                    @pl.when(last if of_right else first)
                    def _():
                        entry.keep(of_right).wait()

            def whole():
                core_final(entry.n, core).start()
                if not deep:
                    own_final(entry.n).start()

            if entry.kind == "C":
                pl.when(entry.piece == 1)(whole)
            else:
                whole()

        def from_sibling(entry):
            def whole():
                core_final(entry.n, 1 - core).wait_recv()
                core_final(entry.n, core).wait_send()
                if not deep:
                    own_final(entry.n).wait()

            for to_right in (True, False):
                end = last if to_right else first
                head = first if to_right else last

                @pl.when(jnp.logical_not(end))
                def _():
                    entry.chain_copy(to_right)[0].wait_send()

                @pl.when(jnp.logical_not(head))
                def _():
                    entry.spread_copy(entry.rows_of(to_right), to_right).wait_send()

                if entry.kind != "B":
                    entry.y_final(entry.rows_of(to_right), to_right).wait_send()
            if entry.kind != "B":
                entry.y_copy(128 - ya + entry.base)[0].wait_send()
            if entry.kind == "C":
                pl.when(entry.piece == 1)(whole)
            else:
                whole()

        for kind in kinds:
            at_entry(kind, s - 2 * nz, True, landed)
        for kind in kinds:
            at_entry(kind, s - (2 * nz + 1), True, from_sibling)

    @pl.loop(0, 8)
    def _(u):
        e = lax.div(u, 2)
        f = lax.rem(u, 2)
        chunk = rows(f, 512)

        @pl.when(f == 0)
        def _():
            @pl.loop(0, images)
            def _(i):
                r = rows(i, PAD)
                og_ref[r, :] = (column(wts_ref[r, :], e) * gp_ref[r, :]).astype(BF)

        def inner(m):
            r = pl.ds(m * 416, 416)
            for c in range(2):
                cols = pl.ds(pl.multiple_of(f * 512 + c * 256, 256), 256)
                pre = dot(xs_ref[r, :], win_ref[e, :, cols]) + ib_ref[pl.ds(e, 1), cols]
                sq = pre * pre
                arg = pre * (0.7978845608028654 + 0.035677408136300125 * sq)
                th = jnp.tanh(arg)
                half = 0.5 + 0.5 * th
                act = pre * half
                h_ref[r, pl.ds(c * 256, 256)] = act.astype(BF)
                slope = 1.5957691216057308 + 0.21406444881780074 * sq
                dg_ref[e, r, cols] = (half + act * (1.0 - half) * slope).astype(BF)

        def outer(m):
            r = pl.ds(m * 416, 416)
            eo = dot(h_ref[r, :], wout_ref[e, chunk, :])
            comb_ref[r, :] += column(wts_ref[r, :], e) * eo
            product = jnp.sum(gp_ref[r, :] * eo, axis=1, keepdims=True)
            gate_ref[r, :] += jnp.where(iota((416, LANES), 1) == e, product, 0.0)

        inner(0)
        for m in range(1, tiles):
            inner(m)
            outer(m - 1)
        outer(tiles - 1)

        @pl.when(u >= 2)
        def _():
            exchange_sib(u - 2).wait_send()

        sib_ref[lax.rem(u, 2)] = dot_tn(h_ref[:, rows(1 - core, 256)], og_ref[...])

        @pl.when(u >= 1)
        def _():
            absorb(u - 1)

        exchange_sib(u).start()
        acc_ref[lax.rem(u, held)] = dot_tn(h_ref[:, rows(core, 256)], og_ref[...])

        @pl.when(f == 1)
        def _():
            service(e)

    gt_ref[...] = jnp.transpose(gate_ref[...])[0:8, :]
    gt_copy = remote(gt_ref, gtl_ref, gt_sem.at[0], gt_sem.at[1], across)
    gt_copy.start()

    def comb_copy(i):
        r = pl.ds(pl.multiple_of(i * PAD, PAD), SENT)
        return remote(comb_ref.at[r, :], combl_hbm.at[r, :], cs_sem.at[i], cr_sem.at[i], across)

    def rg_copy(i):
        r = pl.ds(pl.multiple_of(i * PAD, PAD), SENT)
        return remote(rg_ref.at[r, :], rgl_hbm.at[r, :], rgs_sem.at[i], rgr_sem.at[i], across)

    @pl.loop(0, tiles)
    def _(m):
        r = rows(m, 416)

        @pl.loop(0, 4)
        def _(e):
            og_ref[r, :] = (column(wts_ref[r, :], e) * gp_ref[r, :]).astype(BF)
            for c in range(4):
                cols = pl.ds(c * 256, 256)
                hg = dot_nt(og_ref[r, :], wout_ref[e, cols, :])
                pg = (hg * dg_ref[e, r, cols].astype(F32)).astype(BF)
                dg_ref[e, r, cols] = pg
                at = pl.ds(6 + 2 * e + c // 2, 1)
                small_ref[at, pl.ds((c % 2) * 256, 256)] += jnp.sum(
                    pg.astype(F32), axis=0, keepdims=True
                )
            rg_ref[r, :] += dot_nt(dg_ref[e, r, :], win_ref[e])

        rg_copy(2 * m).start()
        rg_copy(2 * m + 1).start()

        @pl.when(m == 0)
        def _():
            absorb(7)

        service(4 + m)

    def qkv_load(i, j):
        return local_copy(
            qkv_hbm.at[j, rows(i, PAD), :], qkvb_ref.at[lax.rem(i, 2), j], qkv_sem.at[lax.rem(i, 2), j]
        )

    def side_load(i, src, cols, k):
        dst = win_ref.at[lax.div(i, 2), rows(lax.rem(i, 2), PAD), cols]
        return local_copy(src.at[rows(i, PAD), :], dst, load_sem.at[k])

    for j in range(3):
        qkv_load(0, j).start()
    gt_copy.wait_recv()
    gt_copy.wait_send()
    gate_ref[...] = jnp.transpose(
        jnp.concatenate([gt_ref[...] + gtl_ref[...], jnp.zeros((LANES - 8, total), F32)], axis=0)
    )

    @pl.loop(0, images)
    def _(i):
        r = rows(i, PAD)
        fetch = [
            local_copy(mid_hbm.at[r, :], bufa_ref, img_sem.at[0]),
            local_copy(xp_hbm.at[r, :], bufb_ref, img_sem.at[1]),
            side_load(i, normed_hbm, pl.ds(256, 512), 0),
            side_load(i, att_hbm, pl.ds(768, 256), 1),
        ]
        for copy in fetch:
            copy.start()

        @pl.when(i >= images // 2)
        def _():
            for k in range(2):
                comb_copy(2 * i - images + k).start()

        @pl.when(i + 1 < images)
        def _():
            for j in range(3):
                qkv_load(i + 1, j).start()

        e = lax.div(i, 2)
        f = lax.rem(i, 2)
        n = 8 + i

        exchange_sib(n - 2).wait_send()
        sib_ref[lax.rem(n, 2)] = dot_tn(xs_ref[:, rows(1 - core, 256)], dg_ref[e, :, rows(f, 512)])
        exchange_sib(n).start()
        acc_ref[lax.rem(n, held)] = dot_tn(xs_ref[:, rows(core, 256)], dg_ref[e, :, rows(f, 512)])
        rg_copy(i).wait_recv()
        late = local_copy(rgl_hbm.at[r, :], bufc_ref, img_sem.at[4])
        late.start()
        for copy in fetch:
            copy.wait()
        for j in range(3):
            qkv_load(i, j).wait()
        packed = wts_ref[r, :]
        low4 = iota(packed.shape, 1) < 4
        router = jnp.where(low4, pltpu.roll(packed, LANES - 4, 1), 0.0)
        kept = jnp.where(low4, pltpu.roll(packed, LANES - 8, 1), 0.0)
        gg = kept * gate_ref[r, :]
        dl = router * (gg - jnp.sum(router * gg, axis=1, keepdims=True))
        unit, inv = norm_stats(bufa_ref[...])
        late.wait()
        real = iota((PAD, 512), 0) < SEQ
        grad = jnp.where(real, rg_ref[r, :] + bufc_ref[...], 0.0)
        for k in range(4):
            grad = grad + dl[:, k : k + 1] * wr_ref[k : k + 1, :]
        routed = xs_ref[r, :]
        for piece in split_three(dl):
            dwr_ref[...] += dot_tn(piece, routed)
        small_ref[2:3, :] += jnp.sum(grad * unit, axis=0, keepdims=True)
        small_ref[3:4, :] += jnp.sum(grad, axis=0, keepdims=True)
        middle_grad = gp_ref[r, :] + norm_back(grad, g2_ref[...], unit, inv)
        bufa_ref[...] = middle_grad
        branch = middle_grad.astype(BF)
        og_ref[r, :] = branch
        small_ref[4:5, :] += jnp.sum(branch.astype(F32), axis=0, keepdims=True)
        slot = lax.rem(i, 2)
        four = lax.div(i, 4)
        four_rows = rows(lax.rem(i, 4), PAD)
        two_rows = rows(lax.rem(i, 2), PAD)
        for p in range(4):
            cols = pl.ds(p * LANES, LANES)
            weights = (wo_ref if p < 2 else woo_ref)[pl.ds((p % 2) * LANES, LANES), :]
            a_wide = two_heads(dot_nt(branch, weights).astype(BF))
            keys = qkvb_ref[slot, 1, :, cols]
            q_wide = two_heads(qkvb_ref[slot, 0, :, cols])
            probs = pair_probs(keys, q_wide)
            dv = dot(probs.astype(BF), a_wide).astype(BF)
            dpr = dot_nt(qkvb_ref[slot, 2, :, cols], a_wide)
            ds = (probs * (dpr - jnp.sum(dpr * probs, axis=0, keepdims=True))).astype(BF)
            dk = dot(ds, q_wide).astype(BF)
            dq = (one_pair(dot_tn(keys, ds)) * SCALE).astype(BF)
            wout_ref[2, pl.ds(0, PAD), cols] = dq
            wout_ref[2, pl.ds(PAD, PAD), cols] = dk
            wout_ref[2, pl.ds(2 * PAD, PAD), cols] = dv
            if p < 2:
                wout_ref[four, four_rows, cols] = dq
                wout_ref[four, four_rows, pl.ds(256 + p * LANES, LANES)] = dk
                win_ref[lax.div(i, 2), two_rows, cols] = dv
        absorb(n)
        service(n)
        ngrad = jnp.zeros((PAD, 512), F32)
        for j in range(3):
            d = wout_ref[2, pl.ds(j * PAD, PAD), :]
            ngrad += dot_nt(d[:, 0:256], wqkv_ref[j]) + dot_nt(d[:, 256:512], wqo_ref[j])
        q_own = wout_ref[2, pl.ds(0, PAD), 0:256].astype(F32)
        v_own = wout_ref[2, pl.ds(2 * PAD, PAD), 0:256].astype(F32)
        small_ref[5:6, 0:256] += jnp.sum(q_own, axis=0, keepdims=True)
        small_ref[5:6, 256:512] += jnp.sum(v_own, axis=0, keepdims=True)
        unit, inv = norm_stats(bufb_ref[...])
        small_ref[0:1, :] += jnp.sum(ngrad * unit, axis=0, keepdims=True)
        small_ref[1:2, :] += jnp.sum(ngrad, axis=0, keepdims=True)
        result = bufa_ref[...] + norm_back(ngrad, g1_ref[...], unit, inv)
        gp_ref[r, :] = result

    @pl.loop(0, images)
    def _(i):
        rg_copy(i).wait_send()

    close_up(gp_ref, images)
    grad_save = local_copy(gp_ref.at[flat_rows, :], grad_hbm, save_sem.at[0])
    grad_save.start()
    small_ref[14:18, :] = dwr_ref[0:4, :]

    def small_copy(d):
        return remote(
            small_ref,
            smalls_hbm.at[dp],
            sms_sem.at[d],
            smr_sem.at[d],
            {"dp": lax.rem(dp + d, n_dp)},
        )

    small_own = local_copy(small_ref, smalls_hbm.at[dp], sms_sem.at[0])
    small_own.start()

    @pl.loop(1, n_dp)
    def _(d):
        small_copy(d).start()

    def over_images(left_of, right_of):
        return sum(dot_tn(left_of(b), right_of(b)) for b in range(images // 2))

    def normed_of(c):
        cols = pl.ds(pl.multiple_of(256 + c * 256, 256), 256)
        return lambda b: win_ref[b, pl.ds(0, 416), cols]

    def qk_of(k):
        return lambda b: wout_ref[b // 2, pl.ds((b % 2) * 416, 416), pl.ds(k * 256, 256)]

    def query_key(c, dst):
        dst[:, 0:256] = over_images(normed_of(c), qk_of(0))
        dst[:, 256:512] = over_images(normed_of(c), qk_of(1))

    def value_out(c, dst):
        dst[:, 0:256] = over_images(normed_of(c), lambda b: win_ref[b, pl.ds(0, 416), pl.ds(0, 256)])
        dst[:, 256:512] = over_images(
            lambda b: win_ref[b, pl.ds(0, 416), pl.ds(768, 256)],
            lambda b: og_ref[pl.ds(b * 416, 416), rows(c, 256)],
        )

    for n, fill in ((16, query_key), (17, value_out)):
        exchange_sib(n - 2).wait_send()
        fill(1 - core, sib_ref.at[n % 2])
        exchange_sib(n).start()
        fill(core, acc_ref.at[n % held])
        absorb(n)
        if n == 16:
            service(16, "ABC")
            service(17, "ABC")

    @pl.loop(0, images)
    def _(i):
        r = rows(i, PAD)
        service(18 + i, "ABC")
        comb_copy(i).wait_recv()
        fetch = [
            local_copy(mid_hbm.at[r, :], bufa_ref, img_sem.at[0]),
            local_copy(combl_hbm.at[r, :], bufb_ref, img_sem.at[1]),
        ]
        for copy in fetch:
            copy.start()
        comb_copy(i).wait_send()
        for copy in fetch:
            copy.wait()
        result = bufa_ref[...] + (comb_ref[r, :] + bufb_ref[...])
        comb_ref[r, :] = result

    close_up(comb_ref, images)
    layer_save = local_copy(comb_ref.at[flat_rows, :], layer_hbm, save_sem.at[1])
    layer_save.start()

    smallsum_ref[...] = jnp.zeros_like(smallsum_ref)
    small_own.wait()

    @pl.loop(1, n_dp)
    def _(d):
        source = lax.rem(dp + n_dp - d, n_dp)
        remote(small_ref, smalls_hbm.at[source], sms_sem.at[d], smr_sem.at[d], sibling).wait_recv()

    @pl.loop(0, n_dp // 16)
    def _(g):
        copy = local_copy(smalls_hbm.at[rows(g, 16)], sm_ref, img_sem.at[2])
        copy.start()
        copy.wait()

        @pl.loop(0, 16)
        def _(d):
            smallsum_ref[...] += sm_ref[d]

    @pl.loop(18 + images, FIRST_ATT + 3 + 2 * nz + 2)
    def _(s):
        service(s, "ABC")

    @pl.loop(1, n_dp)
    def _(d):
        small_copy(d).wait_send()

    for n in (16, 17):
        exchange_sib(n).wait_send()

    grad_save.wait()
    layer_save.wait()


def finish_kernel(
    units_hbm,
    layer_in,
    grad_in,
    small_ref,
    layer_out,
    grad_out,
    g1_ref,
    b1_ref,
    dwqkv_hbm,
    qvb_ref,
    dwo_hbm,
    ob_ref,
    g2_ref,
    b2_ref,
    dwr_ref,
    dwin_hbm,
    dib_ref,
    dwout_hbm,
    sem,
    *stages,
):
    pairs = []
    for e in range(4):
        for f in range(2):
            chunk = pl.ds(f * 512, 512)
            pairs.append((units_hbm.at[2 * e + f], dwout_hbm.at[e, chunk, :]))
            pairs.append((units_hbm.at[8 + 2 * e + f], dwin_hbm.at[e, :, chunk]))
    low, high = pl.ds(0, 256), pl.ds(256, 256)
    pairs += [
        (units_hbm.at[16, :, low], dwqkv_hbm.at[0]),
        (units_hbm.at[16, :, high], dwqkv_hbm.at[1]),
        (units_hbm.at[17, :, low], dwqkv_hbm.at[2]),
        (units_hbm.at[17, low, high], dwo_hbm.at[:, low]),
        (units_hbm.at[17, high, high], dwo_hbm.at[:, high]),
        (layer_in, layer_out),
        (grad_in, grad_out),
    ]
    ins = [
        pltpu.make_async_copy(src, stages[k], sem.at[0, k]) for k, (src, _) in enumerate(pairs)
    ]
    results = [
        pltpu.make_async_copy(stages[k], dst, sem.at[1, k]) for k, (_, dst) in enumerate(pairs)
    ]
    for copy in ins:
        copy.start()
    g1_ref[...] = small_ref[0:1, :]
    b1_ref[...] = small_ref[1:2, :]
    g2_ref[...] = small_ref[2:3, :]
    b2_ref[...] = small_ref[3:4, :]
    ob_ref[...] = small_ref[4:5, :]
    qvb_ref[0:1, :] = small_ref[5:6, 0:256]
    qvb_ref[1:2, :] = small_ref[5:6, 256:512]
    for e in range(4):
        for f in range(2):
            k = 6 + 2 * e + f
            dib_ref[e : e + 1, pl.ds(f * 512, 512)] = small_ref[k : k + 1, :]
    dwr_ref[...] = small_ref[14:18, :]
    for copy_in, copy_out in zip(ins, results):
        copy_in.wait()
        copy_out.start()
    for copy in results:
        copy.wait()


def local(
    layer_input,
    cotangent,
    ln1_gain,
    ln1_shift,
    w_qkv,
    qv_bias,
    w_out,
    out_bias,
    ln2_gain,
    ln2_shift,
    w_router,
    w_in,
    in_bias,
    w_hidden_out,
    choices,
    priority,
    *,
    n_dp,
):
    tokens, width = layer_input.shape
    experts = w_in.shape[0]
    capacity = (5 * tokens + 2 * experts - 1) // (2 * experts)
    images = tokens // SEQ
    total = images * PAD
    sds = jax.ShapeDtypeStruct
    vmem = pl.BlockSpec(memory_space=pltpu.VMEM)
    hbm = pl.BlockSpec(memory_space=pl.ANY)
    row = lambda v: v.reshape(1, -1)
    dma = pltpu.SemaphoreType.DMA
    block = (128, width)
    outs = pl.pallas_call(
        functools.partial(main_kernel, n_dp, images, capacity),
        out_shape=(
            sds((UNITS, 512, 512), F32),
            sds((tokens, width), F32),
            sds((tokens, width), F32),
            sds((SMALL, width), F32),
            sds((total, width), F32),
            sds((total, width), F32),
            sds((3, total, width), BF),
            sds((total, width), BF),
            sds((total, 256), BF),
            sds((total, width), F32),
            sds((total, width), F32),
            sds((n_dp, SMALL, width), F32),
        ),
        in_specs=[hbm, hbm] + [vmem] * 11 + [hbm, vmem, hbm],
        out_specs=(hbm, hbm, hbm, vmem) + (hbm,) * 8,
        scratch_shapes=[
            pltpu.VMEM((total, width), BF),
            pltpu.VMEM((total, width), F32),
            pltpu.VMEM((total, LANES), F32),
            pltpu.VMEM(w_in.shape, BF),
            pltpu.VMEM(w_hidden_out.shape, BF),
            pltpu.VMEM((total, width), BF),
            pltpu.VMEM((total, width), BF),
            pltpu.VMEM((experts, total, 1024), BF),
            pltpu.VMEM((total, width), F32),
            pltpu.VMEM((total, width), F32),
            pltpu.VMEM((total, LANES), F32),
            pltpu.VMEM((12 if n_dp <= 16 else UNITS, 256, width), F32),
            pltpu.VMEM((2, 256, width), F32),
            pltpu.VMEM((2, 256, width), F32),
            pltpu.VMEM((4,) + block, F32),
            pltpu.VMEM((SLOTS,) + block, F32),
            pltpu.VMEM((SLOTS,) + block, F32),
            pltpu.VMEM((FINALS if n_dp <= 16 else 1, 256, width), F32),
            pltpu.VMEM((8, total), F32),
            pltpu.VMEM((8, total), F32),
            pltpu.VMEM((SMALL, width), F32),
            pltpu.VMEM((16, SMALL, width), F32),
            pltpu.VMEM((LANES, width), F32),
            pltpu.VMEM(w_qkv.shape, BF),
            pltpu.VMEM(w_out.shape, BF),
            pltpu.VMEM(qv_bias.shape, F32),
            pltpu.VMEM((2, 3, PAD, width), BF),
            pltpu.VMEM((PAD, width), F32),
            pltpu.VMEM((PAD, width), F32),
            pltpu.VMEM((PAD, width), F32),
            dma((9,)),
            dma((7,)),
            dma((2, 2)),
            dma((2, 2)),
            dma((2, 4)),
            dma((2,)),
            dma((2, 3)),
            dma((5,)),
            dma((images,)),
            dma((images,)),
            dma((images,)),
            dma((images,)),
            dma((2,)),
            dma((2,)),
            dma((2,)),
        ]
        + [dma((ENTRIES,)) for _ in range(14)]
        + [dma((UNITS,)), dma((UNITS,)), dma((UNITS,)), dma((ENTRIES,))]
        + [
            dma((n_dp,)),
            dma((n_dp,)),
            pltpu.SemaphoreType.REGULAR,
            pltpu.SemaphoreType.REGULAR,
        ],
        compiler_params=pltpu.CompilerParams(
            collective_id=1, has_side_effects=True, vmem_limit_bytes=63 * MIB
        ),
        name="layer",
    )(
        layer_input,
        cotangent,
        choices.T,
        priority,
        row(ln1_gain),
        row(ln1_shift),
        w_qkv,
        qv_bias,
        w_out,
        row(out_bias),
        row(ln2_gain),
        row(ln2_shift),
        w_router.T,
        w_in,
        in_bias,
        w_hidden_out,
    )
    units, layer_out, input_grad, small = outs[:4]
    vector = sds((1, width), F32)
    results = pl.pallas_call(
        finish_kernel,
        out_shape=(
            sds(layer_input.shape, F32),
            sds(layer_input.shape, F32),
            vector,
            vector,
            sds(w_qkv.shape, F32),
            sds(qv_bias.shape, F32),
            sds(w_out.shape, F32),
            vector,
            vector,
            vector,
            sds(w_router.shape[::-1], F32),
            sds(w_in.shape, F32),
            sds(in_bias.shape, F32),
            sds(w_hidden_out.shape, F32),
        ),
        in_specs=[hbm, hbm, hbm, vmem],
        out_specs=(hbm, hbm, vmem, vmem, hbm, vmem, hbm, vmem, vmem, vmem, vmem, hbm, vmem, hbm),
        scratch_shapes=[dma((2, 23))]
        + [pltpu.VMEM((512, 512), F32)] * 16
        + [pltpu.VMEM((512, 256), F32)] * 3
        + [pltpu.VMEM((256, 256), F32)] * 2
        + [pltpu.VMEM((tokens, width), F32)] * 2,
        compiler_params=pltpu.CompilerParams(vmem_limit_bytes=62 * MIB),
        name="finish",
    )(units, layer_out, input_grad, small)
    results = [v.reshape(width) if v.shape == (1, width) else v for v in results]
    results[10] = results[10].T
    return tuple(results)


def solution(mesh):
    whole = P()
    placed = (
        P("dp", None),
        P("dp", None),
        whole,
        whole,
        P(None, None, "tensor"),
        P(None, "tensor"),
        P("tensor", None),
        whole,
        whole,
        whole,
        whole,
        P(None, None, "tensor"),
        P(None, "tensor"),
        P(None, "tensor", None),
        P("dp", None),
        P("dp", None),
    )
    grads = placed[2:14]
    return jax.shard_map(
        functools.partial(local, n_dp=mesh.shape["dp"]),
        mesh=mesh,
        in_specs=placed,
        out_specs=(P("dp", None), P("dp", None)) + grads,
        check_vma=False,
    )
```

```python
import functools

import jax
import jax.numpy as jnp
from jax import lax
from jax.experimental import pallas as pl
from jax.experimental.pallas import tpu as pltpu
from jax.sharding import PartitionSpec as P

HEAD_DIM = 64
SEQ = 197
PAD = 208
SENT = 200
LANES = 128
EPS = 1e-06
SCALE = HEAD_DIM ** (-0.5)
BF = jnp.bfloat16
F32 = jnp.float32
MESH = pl.DeviceIdType.MESH
MIB = 1 << 20

UNITS = 18
ENTRIES = 20
SLOTS = 4
FINALS = 8
FIRST_ATT = 16
SMALL = 24


def dot(a, b):
    return jnp.dot(a, b, preferred_element_type=F32)


def dot_nt(a, b):
    return lax.dot_general(a, b, (((1,), (1,)), ((), ())), preferred_element_type=F32)


def dot_tn(a, b):
    return lax.dot_general(a, b, (((0,), (0,)), ((), ())), preferred_element_type=F32)


def rows(i, size):
    return pl.ds(pl.multiple_of(i * size, size), size)


def span(start, size):
    return pl.ds(pl.multiple_of(start, 32), size)


def iota(shape, axis):
    return lax.broadcasted_iota(jnp.int32, shape, axis)


def column(vals, index):
    return jnp.sum(jnp.where(iota(vals.shape, 1) == index, vals, 0.0), axis=1, keepdims=True)


def norm_stats(vals):
    centred = vals - jnp.mean(vals, axis=1, keepdims=True)
    inv = lax.rsqrt(jnp.mean(centred * centred, axis=1, keepdims=True) + EPS)
    return centred * inv, inv


def norm_back(grad, gain, unit, inv):
    scaled = grad * gain
    mean_one = jnp.mean(scaled, axis=1, keepdims=True)
    mean_two = jnp.mean(scaled * unit, axis=1, keepdims=True)
    return inv * (scaled - mean_one - unit * mean_two)


def split_three(vals):
    high = vals.astype(BF)
    rest = vals - high.astype(F32)
    mid = rest.astype(BF)
    low = (rest - mid.astype(F32)).astype(BF)
    return high, mid, low


def spread(flat_ref, padded_ref, images):
    for i in range(images):
        padded_ref[pl.ds(i * PAD + PAD - 16, 16), :] = jnp.zeros((16, padded_ref.shape[1]), F32)
        padded_ref[pl.ds(i * PAD, SEQ), :] = flat_ref[pl.ds(i * SEQ, SEQ), :]


def close_up(ref, images):
    for i in range(1, images):
        ref[pl.ds(i * SEQ, SEQ), :] = ref[pl.ds(i * PAD, SEQ), :]


def two_heads(pair):
    low = iota(pair.shape, 1) < HEAD_DIM
    zero = jnp.zeros_like(pair)
    gap = jnp.zeros((256 - PAD, LANES), pair.dtype)
    return jnp.concatenate([jnp.where(low, pair, zero), gap, jnp.where(low, zero, pair), gap], axis=0)


def one_pair(wide):
    merged = jnp.where(iota((LANES, 256), 0) < HEAD_DIM, wide[:, 0:256], wide[:, 256:512])
    return jnp.transpose(merged)[0:PAD]


def pair_probs(keys, q_wide):
    scores = dot_nt(keys, q_wide)
    tail = scores[PAD - 16 :]
    tail = jnp.where(iota(tail.shape, 0) < SEQ - (PAD - 16), tail, -1e30)
    scores = jnp.concatenate([scores[: PAD - 16], tail], axis=0)
    exps = jnp.exp(scores - jnp.max(scores, axis=0, keepdims=True))
    return exps * (1.0 / jnp.sum(exps, axis=0, keepdims=True))


def main_kernel(
    n_dp,
    images,
    capacity,
    x_hbm,
    cot_hbm,
    choice_ref,
    prio_ref,
    g1_ref,
    b1_ref,
    wqkv_ref,
    qvb_ref,
    wo_ref,
    ob_ref,
    g2_ref,
    b2_ref,
    wr_ref,
    win_hbm,
    ib_ref,
    wout_hbm,
    out_hbm,
    layer_hbm,
    grad_hbm,
    smallsum_ref,
    rgl_hbm,
    combl_hbm,
    qkv_hbm,
    normed_hbm,
    att_hbm,
    mid_hbm,
    xp_hbm,
    smalls_hbm,
    xs_ref,
    gp_ref,
    wts_ref,
    win_ref,
    wout_ref,
    og_ref,
    h_ref,
    dg_ref,
    comb_ref,
    rg_ref,
    gate_ref,
    acc_ref,
    sib_ref,
    landc_ref,
    landy_ref,
    landr_ref,
    landl_ref,
    fin_ref,
    gt_ref,
    gtl_ref,
    small_ref,
    sm_ref,
    dwr_ref,
    wqo_ref,
    woo_ref,
    bias_ref,
    qkvb_ref,
    bufa_ref,
    bufb_ref,
    bufc_ref,
    load_sem,
    save_sem,
    fx_sem,
    fy_sem,
    fs_sem,
    fb_sem,
    qkv_sem,
    img_sem,
    rgs_sem,
    rgr_sem,
    cs_sem,
    cr_sem,
    gt_sem,
    sib_sem,
    landc_sem,
    ys_sem,
    yr_sem,
    rs_sem,
    rr_sem,
    ls_sem,
    lr_sem,
    brs_sem,
    brr_sem,
    bls_sem,
    blr_sem,
    ars_sem,
    arr_sem,
    als_sem,
    alr_sem,
    ks_sem,
    kr_sem,
    kl_sem,
    loc_sem,
    sms_sem,
    smr_sem,
    credit_r,
    credit_l,
):
    total = images * PAD
    flat = images * SEQ
    tiles = total // 416
    nz = n_dp // 4
    deep = nz > 4
    held = acc_ref.shape[0]
    dp = lax.axis_index("dp")
    tensor = lax.axis_index("tensor")
    core = lax.rem(dp, 2)
    y = lax.rem(lax.div(dp, 2), 2)
    z = lax.div(dp, 4)
    across = {"tensor": 1 - tensor}
    sibling = {"dp": dp + 1 - 2 * core}
    ypal = {"dp": dp + 2 - 4 * y}
    right = {"dp": lax.rem(dp + 4, n_dp)}
    left = {"dp": lax.rem(dp + n_dp - 4, n_dp)}
    first, last = z == 0, z == nz - 1

    def remote(src, dst, send, recv, where):
        return pltpu.make_async_remote_copy(src, dst, send, recv, where, MESH)

    def local_copy(src, dst, sem):
        return pltpu.make_async_copy(src, dst, sem)

    flat_rows = pl.ds(0, flat)
    x_load = local_copy(x_hbm, comb_ref.at[flat_rows, :], load_sem.at[8])
    x_load.start()
    weight_loads = []
    for e in range(4):
        weight_loads.append(local_copy(win_hbm.at[e], win_ref.at[e], load_sem.at[e]))
        weight_loads.append(local_copy(wout_hbm.at[e], wout_ref.at[e], load_sem.at[4 + e]))
    barrier = pltpu.get_barrier_semaphore()
    pl.semaphore_signal(barrier, inc=1, device_id=across, device_id_type=MESH)

    @pl.loop(1, n_dp)
    def _(d):
        pl.semaphore_signal(
            barrier, inc=1, device_id={"dp": lax.rem(dp + d, n_dp)}, device_id_type=MESH
        )

    def land(j, half):
        return acc_ref.at[j, :, rows(half, 256)]

    half_rows = rows(core, 256)

    @pl.when(y == 0)
    def _():
        acc_ref[4, :, 0:256] = wqkv_ref[0, half_rows, :].astype(F32)
        acc_ref[5, :, 0:256] = wqkv_ref[2, half_rows, :].astype(F32)

    @pl.when(y == 1)
    def _():
        acc_ref[4, :, 0:256] = wqkv_ref[1, half_rows, :].astype(F32)
        acc_ref[5, :, 0:256] = wo_ref[:, half_rows].astype(F32)

    pl.semaphore_wait(barrier, n_dp)

    def fetch_x(t):
        src = acc_ref.at[4 + t, :, pl.ds(0, 256)]
        return remote(src, land(y + 2 * t, core), fx_sem.at[0, t], fx_sem.at[1, t], across)

    def fetch_y(t, mine):
        j = (y if mine else 1 - y) + 2 * t
        return remote(land(j, core), land(j, core), fy_sem.at[0, t], fy_sem.at[1, t], ypal)

    def fetch_sib(j, half):
        return remote(land(j, half), land(j, half), fs_sem.at[0, j], fs_sem.at[1, j], sibling)

    for t in range(2):
        fetch_x(t).start()
    fetch_bias = remote(qvb_ref, bias_ref, fb_sem.at[0], fb_sem.at[1], across)
    fetch_bias.start()
    for copy in weight_loads:
        copy.start()

    x_load.wait()
    spread(comb_ref, rg_ref, images)
    cot_load = local_copy(cot_hbm, comb_ref.at[flat_rows, :], load_sem.at[8])
    cot_load.start()
    xp_save = local_copy(rg_ref, xp_hbm, save_sem.at[0])
    xp_save.start()
    n_cols = pl.ds(512, 512)

    @pl.loop(0, images)
    def _(i):
        r = rows(i, PAD)
        unit, _ = norm_stats(rg_ref[r, :])
        dg_ref[3, r, n_cols] = (unit * g1_ref[...] + b1_ref[...]).astype(BF)

    normed_save = local_copy(dg_ref.at[3, :, n_cols], normed_hbm, save_sem.at[1])
    normed_save.start()

    def qkv_view(j, side):
        return (0, 0, 1)[j], (0, 512, 0)[j] + side * 256

    def project(side, weights, biases):
        @pl.loop(0, tiles)
        def _(m):
            r = rows(m, 416)
            for j in range(3):
                out = dot(dg_ref[3, r, n_cols], weights[j])
                if j == 0:
                    out = (out + biases[0:1, :]) * SCALE
                if j == 2:
                    out = out + biases[1:2, :]
                a, c = qkv_view(j, side)
                dg_ref[a, r, pl.ds(c, 256)] = out.astype(BF)

    def attend(side, start, stop):
        @pl.loop(start, stop)
        def _(i):
            r = rows(i, PAD)
            for p in range(2):
                c = side * 256 + p * LANES
                probs = pair_probs(
                    dg_ref[0, r, pl.ds(512 + c, LANES)], two_heads(dg_ref[0, r, pl.ds(c, LANES)])
                )
                wide = dot_tn(dg_ref[1, r, pl.ds(c, LANES)], probs.astype(BF))
                h_ref[r, pl.ds(c, LANES)] = one_pair(wide).astype(BF)

    project(0, wqkv_ref, qvb_ref)
    attend(0, 0, images // 2)
    for t in range(2):
        fetch_x(t).wait_recv()
        fetch_y(t, True).start()
        fetch_sib(y + 2 * t, core).start()
    attend(0, images // 2, images)
    for t in range(2):
        fetch_y(t, False).wait_recv()
        fetch_sib(1 - y + 2 * t, core).start()

    gt_ref[...] = jnp.full(gt_ref.shape, 1e6, F32)
    gt_ref[0:2, 0:flat] = choice_ref[...].astype(F32)
    gt_ref[2:3, 0:flat] = prio_ref[...].astype(F32)
    gate_ref[:, 0:8] = jnp.transpose(gt_ref[...])
    lane = iota((total, LANES), 1).astype(F32)
    hot0 = (gate_ref[:, 0:1] == lane).astype(F32)
    og_ref[:, 0:128] = hot0.astype(BF)
    og_ref[:, 128:256] = (gate_ref[:, 1:2] == lane).astype(F32).astype(BF)
    total0 = jnp.sum(hot0, axis=0, keepdims=True)

    @pl.loop(0, images)
    def _(i):
        own = gate_ref[pl.ds(i * SEQ, PAD), :]
        lane_r = iota((PAD, LANES), 1).astype(F32)
        earlier = (gt_ref[2:3, :] < own[:, 2:3]).astype(F32).astype(BF)
        pos = dot(earlier, og_ref[:, 0:256])
        kept0 = (own[:, 0:1] == lane_r) & (pos[:, 0:128] < capacity)
        kept1 = (own[:, 1:2] == lane_r) & (pos[:, 128:256] + total0 < capacity)
        real = iota((PAD, LANES), 0) < SEQ
        wts_ref[rows(i, PAD), :] = jnp.where((kept0 | kept1) & real, 1.0, 0.0)

    cot_load.wait()
    spread(comb_ref, gp_ref, images)

    wr_wide = jnp.transpose(
        jnp.concatenate([wr_ref[...], jnp.zeros((LANES - 4, wr_ref.shape[1]), F32)], axis=0)
    )
    wr_parts = split_three(wr_wide)

    fetch_bias.wait_recv()
    for j in range(4):
        fetch_sib(j, 1 - core).wait_recv()
    for j in range(3):
        wqo_ref[j, 0:256, :] = acc_ref[j, :, 0:256].astype(BF)
        wqo_ref[j, 256:512, :] = acc_ref[j, :, 256:512].astype(BF)
    woo_ref[...] = acc_ref[3].astype(BF)
    project(1, wqo_ref, bias_ref)
    qkv_saves = []
    for j in range(3):
        a, c = qkv_view(j, 0)
        qkv_saves.append(local_copy(dg_ref.at[a, :, pl.ds(c, 512)], qkv_hbm.at[j], save_sem.at[2 + j]))
        qkv_saves[-1].start()
    attend(1, 0, images)
    att_save = local_copy(h_ref.at[:, pl.ds(0, 256)], att_hbm, save_sem.at[5])
    att_save.start()

    @pl.loop(0, tiles)
    def _(m):
        r = rows(m, 416)
        branch = dot(h_ref[r, 0:256], wo_ref[...]) + dot(h_ref[r, 256:512], woo_ref[...])
        middle = rg_ref[r, :] + (branch + ob_ref[...])
        comb_ref[r, :] = middle
        unit, _ = norm_stats(middle)
        routed = (unit * g2_ref[...] + b2_ref[...]).astype(BF)
        xs_ref[r, :] = routed
        logits = dot(routed, wr_parts[0]) + dot(routed, wr_parts[1]) + dot(routed, wr_parts[2])
        logits = jnp.where(iota(logits.shape, 1) < 4, logits, -1e30)
        exps = jnp.exp(logits - jnp.max(logits, axis=1, keepdims=True))
        router = exps / jnp.sum(exps, axis=1, keepdims=True)
        kept = wts_ref[r, :]
        wts_ref[r, :] = (
            kept * router.astype(BF).astype(F32) + pltpu.roll(router, 4, 1) + pltpu.roll(kept, 8, 1)
        )

    mid_save = local_copy(comb_ref, mid_hbm, save_sem.at[6])
    mid_save.start()
    gate_ref[...] = jnp.zeros_like(gate_ref)
    small_ref[...] = jnp.zeros_like(small_ref)
    dwr_ref[...] = jnp.zeros_like(dwr_ref)
    for copy in weight_loads:
        copy.wait()
    for t in range(2):
        fetch_x(t).wait_send()
        fetch_y(t, True).wait_send()
    for j in range(4):
        fetch_sib(j, core).wait_send()
    fetch_bias.wait_send()
    for copy in [xp_save, normed_save, att_save, mid_save] + qkv_saves:
        copy.wait()
    comb_ref[...] = jnp.zeros_like(comb_ref)
    rg_ref[...] = jnp.zeros_like(rg_ref)

    def place(n, start, size):
        return out_hbm.at[n, span(core * 256 + start, size), :]

    def slot_of(n):
        return n - jnp.where(n >= held, held, 0)

    def part(n, start, size):
        return acc_ref.at[slot_of(n), span(start, size), :]

    def add(n, start, size, land_ref):
        acc_ref[slot_of(n), span(start, size), :] += land_ref[...]

    def final(n, start, size):
        if deep:
            return place(n, start, size)
        return fin_ref.at[lax.rem(n, FINALS), span(start, size), :]

    def exchange_sib(n):
        slot = lax.rem(n, 2)
        return remote(
            sib_ref.at[slot], landc_ref.at[slot], sib_sem.at[slot], landc_sem.at[slot], sibling
        )

    def absorb(n):
        exchange_sib(n).wait_recv()
        acc_ref[slot_of(n)] += landc_ref[lax.rem(n, 2)]

    ya = y * 128

    class Entry:
        def __init__(self, kind, v):
            self.kind = kind
            if kind == "C":
                self.there = (v >= FIRST_ATT) & (v < FIRST_ATT + 4)
                self.q = v - FIRST_ATT + 16
                self.n = 16 + lax.div(self.q - 16, 2)
                self.piece = lax.rem(self.q, 2)
                self.yrows = 64
                self.base = self.piece * 64
                self.turn = lax.rem(self.q, 2)
            else:
                self.there = (v >= 0) & (v < 16) & (lax.rem(v, 2) == (0 if kind == "A" else 1))
                self.q = v
                self.n = self.q
                self.yrows = 128
                self.base = 0
                self.turn = lax.rem(lax.div(self.q, 2), 2) + (2 if kind == "B" else 0)
            if kind == "B":
                self.right, self.left = (0, 128), (128, 128)
            else:
                size = self.yrows // 2
                self.right = (ya + self.base, size)
                self.left = (ya + self.base + size, size)

        def half(self, to_right):
            return self.right if to_right else self.left

        def y_copy(self, start):
            land_ref = landy_ref.at[self.turn, pl.ds(0, self.yrows), :]
            return remote(
                part(self.n, start, self.yrows), land_ref, ys_sem.at[self.q], yr_sem.at[self.q], ypal
            ), land_ref

        def chain_copy(self, to_right):
            start, size = self.half(to_right)
            land_ref = (landr_ref if to_right else landl_ref).at[
                lax.rem(self.q, SLOTS), pl.ds(0, size), :
            ]
            send, recv = (rs_sem, rr_sem) if to_right else (ls_sem, lr_sem)
            where = right if to_right else left
            return remote(
                part(self.n, start, size), land_ref, send.at[self.q], recv.at[self.q], where
            ), land_ref

        def spread_copy(self, src, of_right):
            send, recv = (brs_sem, brr_sem) if of_right else (bls_sem, blr_sem)
            return remote(
                src, self.spot(of_right), send.at[self.q], recv.at[self.q], left if of_right else right
            )

        def spot(self, of_right):
            return final(self.n, *self.half(of_right))

        def rows_of(self, of_right):
            return part(self.n, *self.half(of_right))

        def y_final(self, src, of_right):
            send, recv = (ars_sem, arr_sem) if of_right else (als_sem, alr_sem)
            return remote(src, self.spot(of_right), send.at[self.q], recv.at[self.q], ypal)

        def y_final_in(self, of_right):
            start, size = self.half(of_right)
            spot = final(self.n, start + 128 - 2 * ya, size)
            send, recv = (ars_sem, arr_sem) if of_right else (als_sem, alr_sem)
            return remote(spot, spot, send.at[self.q], recv.at[self.q], ypal)

        def keep(self, of_right):
            return local_copy(self.rows_of(of_right), self.spot(of_right), loc_sem.at[self.q])

    def core_final(n, half):
        return remote(
            final(n, 0, 256), out_hbm.at[n, rows(half, 256), :], ks_sem.at[n], kr_sem.at[n], sibling
        )

    def own_final(n):
        return local_copy(final(n, 0, 256), place(n, 0, 256), kl_sem.at[n])

    def at_entry(kind, v, cond, body):
        entry = Entry(kind, v)

        @pl.when(entry.there & cond)
        def _():
            body(entry)

    def finish(entry, of_right):
        src = entry.rows_of(of_right)
        if deep:
            entry.keep(of_right).start()
        else:
            start, size = entry.half(of_right)
            fin_ref[lax.rem(entry.n, FINALS), span(start, size), :] = src[...]
            src = entry.spot(of_right)
        entry.spread_copy(src, of_right).start()
        if entry.kind != "B":
            entry.y_final(src, of_right).start()

    def service(s, kinds="AB"):
        for of_right in (True, False):
            source = last if of_right else first
            sink = first if of_right else last
            v = s - nz - ((nz - 1 - z) if of_right else z)

            def passed_on(entry, of_right=of_right, sink=sink):
                here = entry.spot(of_right)
                entry.spread_copy(here, of_right).wait_recv()

                @pl.when(jnp.logical_not(sink))
                def _():
                    entry.spread_copy(here, of_right).start()

                if entry.kind != "B":
                    entry.y_final(here, of_right).start()

            for kind in kinds:
                at_entry(kind, v, jnp.logical_not(source), passed_on)

        def y_in(entry):
            copy, land_ref = entry.y_copy(128 - ya + entry.base)
            copy.wait_recv()
            add(entry.n, ya + entry.base, entry.yrows, land_ref)

        def y_out(entry):
            entry.y_copy(128 - ya + entry.base)[0].start()

        for kind in kinds:
            if kind != "B":
                at_entry(kind, s - 1, True, y_in)
        for kind in kinds:
            if kind != "B":
                at_entry(kind, s, True, y_out)

        for kind in kinds:
            for to_right in (True, False):
                hop = z if to_right else nz - 1 - z
                v = s - hop - (0 if kind == "B" else 1)
                head, end = (first, last) if to_right else (last, first)
                credit = credit_r if to_right else credit_l
                back = left if to_right else right

                def chain(entry, to_right=to_right, head=head, end=end, credit=credit, back=back):
                    copy, land_ref = entry.chain_copy(to_right)
                    start, size = entry.half(to_right)

                    @pl.when(jnp.logical_not(head))
                    def _():
                        copy.wait_recv()
                        add(entry.n, start, size, land_ref)

                        @pl.when(entry.q + SLOTS < ENTRIES)
                        def _():
                            pl.semaphore_signal(credit, inc=1, device_id=back, device_id_type=MESH)

                    @pl.when(jnp.logical_not(end))
                    def _():
                        @pl.when(entry.q >= SLOTS)
                        def _():
                            pl.semaphore_wait(credit, 1)

                        copy.start()

                    @pl.when(end)
                    def _():
                        if entry.kind == "B":
                            entry.y_copy(start)[0].start()
                        else:
                            finish(entry, to_right)

                at_entry(kind, v, True, chain)

        if "B" in kinds:
            for to_right in (True, False):

                def root(entry, to_right=to_right):
                    start, size = entry.half(to_right)
                    copy, land_ref = entry.y_copy(start)
                    copy.wait_send()
                    copy.wait_recv()
                    add(entry.n, start, size, land_ref)
                    finish(entry, to_right)

                at_entry("B", s - nz, last if to_right else first, root)

        def landed(entry):
            for of_right in (True, False):
                if entry.kind != "B":
                    entry.y_final_in(of_right).wait_recv()

                if deep:

                    @pl.when(last if of_right else first)
                    def _():
                        entry.keep(of_right).wait()

            def whole():
                core_final(entry.n, core).start()
                if not deep:
                    own_final(entry.n).start()

            if entry.kind == "C":
                pl.when(entry.piece == 1)(whole)
            else:
                whole()

        def from_sibling(entry):
            def whole():
                core_final(entry.n, 1 - core).wait_recv()
                core_final(entry.n, core).wait_send()
                if not deep:
                    own_final(entry.n).wait()

            for to_right in (True, False):
                end = last if to_right else first
                head = first if to_right else last

                @pl.when(jnp.logical_not(end))
                def _():
                    entry.chain_copy(to_right)[0].wait_send()

                @pl.when(jnp.logical_not(head))
                def _():
                    entry.spread_copy(entry.rows_of(to_right), to_right).wait_send()

                if entry.kind != "B":
                    entry.y_final(entry.rows_of(to_right), to_right).wait_send()
            if entry.kind != "B":
                entry.y_copy(128 - ya + entry.base)[0].wait_send()
            if entry.kind == "C":
                pl.when(entry.piece == 1)(whole)
            else:
                whole()

        for kind in kinds:
            at_entry(kind, s - 2 * nz, True, landed)
        for kind in kinds:
            at_entry(kind, s - (2 * nz + 1), True, from_sibling)

    @pl.loop(0, 8)
    def _(u):
        e = lax.div(u, 2)
        f = lax.rem(u, 2)
        chunk = rows(f, 512)

        @pl.when(f == 0)
        def _():
            @pl.loop(0, images)
            def _(i):
                r = rows(i, PAD)
                og_ref[r, :] = (column(wts_ref[r, :], e) * gp_ref[r, :]).astype(BF)

        def inner(m):
            r = pl.ds(m * 416, 416)
            for c in range(2):
                cols = pl.ds(pl.multiple_of(f * 512 + c * 256, 256), 256)
                pre = dot(xs_ref[r, :], win_ref[e, :, cols]) + ib_ref[pl.ds(e, 1), cols]
                sq = pre * pre
                arg = pre * (0.7978845608028654 + 0.035677408136300125 * sq)
                th = jnp.tanh(arg)
                half = 0.5 + 0.5 * th
                act = pre * half
                h_ref[r, pl.ds(c * 256, 256)] = act.astype(BF)
                slope = 1.5957691216057308 + 0.21406444881780074 * sq
                dg_ref[e, r, cols] = (half + act * (1.0 - half) * slope).astype(BF)

        def outer(m):
            r = pl.ds(m * 416, 416)
            eo = dot(h_ref[r, :], wout_ref[e, chunk, :])
            comb_ref[r, :] += column(wts_ref[r, :], e) * eo
            product = jnp.sum(gp_ref[r, :] * eo, axis=1, keepdims=True)
            gate_ref[r, :] += jnp.where(iota((416, LANES), 1) == e, product, 0.0)

        inner(0)
        for m in range(1, tiles):
            inner(m)
            outer(m - 1)
        outer(tiles - 1)

        @pl.when(u >= 2)
        def _():
            exchange_sib(u - 2).wait_send()

        sib_ref[lax.rem(u, 2)] = dot_tn(h_ref[:, rows(1 - core, 256)], og_ref[...])

        @pl.when(u >= 1)
        def _():
            absorb(u - 1)

        exchange_sib(u).start()
        acc_ref[slot_of(u)] = dot_tn(h_ref[:, rows(core, 256)], og_ref[...])

        @pl.when(f == 1)
        def _():
            service(e)

    gt_ref[...] = jnp.transpose(gate_ref[...])[0:8, :]
    gt_copy = remote(gt_ref, gtl_ref, gt_sem.at[0], gt_sem.at[1], across)
    gt_copy.start()

    def comb_copy(i):
        r = pl.ds(pl.multiple_of(i * PAD, PAD), SENT)
        return remote(comb_ref.at[r, :], combl_hbm.at[r, :], cs_sem.at[i], cr_sem.at[i], across)

    def rg_copy(i):
        r = pl.ds(pl.multiple_of(i * PAD, PAD), SENT)
        return remote(rg_ref.at[r, :], rgl_hbm.at[r, :], rgs_sem.at[i], rgr_sem.at[i], across)

    @pl.loop(0, tiles)
    def _(m):
        r = rows(m, 416)

        @pl.loop(0, 4)
        def _(e):
            og_ref[r, :] = (column(wts_ref[r, :], e) * gp_ref[r, :]).astype(BF)
            for c in range(4):
                cols = pl.ds(c * 256, 256)
                hg = dot_nt(og_ref[r, :], wout_ref[e, cols, :])
                pg = (hg * dg_ref[e, r, cols].astype(F32)).astype(BF)
                dg_ref[e, r, cols] = pg
                at = pl.ds(6 + 2 * e + c // 2, 1)
                small_ref[at, pl.ds((c % 2) * 256, 256)] += jnp.sum(
                    pg.astype(F32), axis=0, keepdims=True
                )
            rg_ref[r, :] += dot_nt(dg_ref[e, r, :], win_ref[e])

        rg_copy(2 * m).start()
        rg_copy(2 * m + 1).start()

        @pl.when(m == 0)
        def _():
            absorb(7)

        service(4 + m)

    def qkv_load(i, j):
        return local_copy(
            qkv_hbm.at[j, rows(i, PAD), :], qkvb_ref.at[lax.rem(i, 2), j], qkv_sem.at[lax.rem(i, 2), j]
        )

    def side_load(i, src, cols, k):
        dst = win_ref.at[lax.div(i, 2), rows(lax.rem(i, 2), PAD), cols]
        return local_copy(src.at[rows(i, PAD), :], dst, load_sem.at[k])

    for j in range(3):
        qkv_load(0, j).start()
    gt_copy.wait_recv()
    gt_copy.wait_send()
    gate_ref[...] = jnp.transpose(
        jnp.concatenate([gt_ref[...] + gtl_ref[...], jnp.zeros((LANES - 8, total), F32)], axis=0)
    )

    @pl.loop(0, images)
    def _(i):
        r = rows(i, PAD)
        fetch = [
            local_copy(mid_hbm.at[r, :], bufa_ref, img_sem.at[0]),
            local_copy(xp_hbm.at[r, :], bufb_ref, img_sem.at[1]),
            side_load(i, normed_hbm, pl.ds(256, 512), 0),
            side_load(i, att_hbm, pl.ds(768, 256), 1),
        ]
        for copy in fetch:
            copy.start()

        @pl.when(i >= images // 2)
        def _():
            for k in range(2):
                comb_copy(2 * i - images + k).start()

        @pl.when(i + 1 < images)
        def _():
            for j in range(3):
                qkv_load(i + 1, j).start()

        e = lax.div(i, 2)
        f = lax.rem(i, 2)
        n = 8 + i

        exchange_sib(n - 2).wait_send()
        sib_ref[lax.rem(n, 2)] = dot_tn(xs_ref[:, rows(1 - core, 256)], dg_ref[e, :, rows(f, 512)])
        exchange_sib(n).start()
        acc_ref[slot_of(n)] = dot_tn(xs_ref[:, rows(core, 256)], dg_ref[e, :, rows(f, 512)])
        rg_copy(i).wait_recv()
        late = local_copy(rgl_hbm.at[r, :], bufc_ref, img_sem.at[4])
        late.start()
        for copy in fetch:
            copy.wait()
        for j in range(3):
            qkv_load(i, j).wait()
        packed = wts_ref[r, :]
        low4 = iota(packed.shape, 1) < 4
        router = jnp.where(low4, pltpu.roll(packed, LANES - 4, 1), 0.0)
        kept = jnp.where(low4, pltpu.roll(packed, LANES - 8, 1), 0.0)
        gg = kept * gate_ref[r, :]
        dl = router * (gg - jnp.sum(router * gg, axis=1, keepdims=True))
        unit, inv = norm_stats(bufa_ref[...])
        late.wait()
        real = iota((PAD, 512), 0) < SEQ
        grad = jnp.where(real, rg_ref[r, :] + bufc_ref[...], 0.0)
        for k in range(4):
            grad = grad + dl[:, k : k + 1] * wr_ref[k : k + 1, :]
        routed = xs_ref[r, :]
        for piece in split_three(dl):
            dwr_ref[...] += dot_tn(piece, routed)
        small_ref[2:3, :] += jnp.sum(grad * unit, axis=0, keepdims=True)
        small_ref[3:4, :] += jnp.sum(grad, axis=0, keepdims=True)
        middle_grad = gp_ref[r, :] + norm_back(grad, g2_ref[...], unit, inv)
        bufa_ref[...] = middle_grad
        branch = middle_grad.astype(BF)
        og_ref[r, :] = branch
        small_ref[4:5, :] += jnp.sum(branch.astype(F32), axis=0, keepdims=True)
        slot = lax.rem(i, 2)
        four = lax.div(i, 4)
        four_rows = rows(lax.rem(i, 4), PAD)
        two_rows = rows(lax.rem(i, 2), PAD)
        for p in range(4):
            cols = pl.ds(p * LANES, LANES)
            weights = (wo_ref if p < 2 else woo_ref)[pl.ds((p % 2) * LANES, LANES), :]
            a_wide = two_heads(dot_nt(branch, weights).astype(BF))
            keys = qkvb_ref[slot, 1, :, cols]
            q_wide = two_heads(qkvb_ref[slot, 0, :, cols])
            probs = pair_probs(keys, q_wide)
            dv = dot(probs.astype(BF), a_wide).astype(BF)
            dpr = dot_nt(qkvb_ref[slot, 2, :, cols], a_wide)
            ds = (probs * (dpr - jnp.sum(dpr * probs, axis=0, keepdims=True))).astype(BF)
            dk = dot(ds, q_wide).astype(BF)
            dq = (one_pair(dot_tn(keys, ds)) * SCALE).astype(BF)
            wout_ref[2, pl.ds(0, PAD), cols] = dq
            wout_ref[2, pl.ds(PAD, PAD), cols] = dk
            wout_ref[2, pl.ds(2 * PAD, PAD), cols] = dv
            if p < 2:
                wout_ref[four, four_rows, cols] = dq
                wout_ref[four, four_rows, pl.ds(256 + p * LANES, LANES)] = dk
                win_ref[lax.div(i, 2), two_rows, cols] = dv
        absorb(n)
        service(n)
        ngrad = jnp.zeros((PAD, 512), F32)
        for j in range(3):
            d = wout_ref[2, pl.ds(j * PAD, PAD), :]
            ngrad += dot_nt(d[:, 0:256], wqkv_ref[j]) + dot_nt(d[:, 256:512], wqo_ref[j])
        q_own = wout_ref[2, pl.ds(0, PAD), 0:256].astype(F32)
        v_own = wout_ref[2, pl.ds(2 * PAD, PAD), 0:256].astype(F32)
        small_ref[5:6, 0:256] += jnp.sum(q_own, axis=0, keepdims=True)
        small_ref[5:6, 256:512] += jnp.sum(v_own, axis=0, keepdims=True)
        unit, inv = norm_stats(bufb_ref[...])
        small_ref[0:1, :] += jnp.sum(ngrad * unit, axis=0, keepdims=True)
        small_ref[1:2, :] += jnp.sum(ngrad, axis=0, keepdims=True)
        result = bufa_ref[...] + norm_back(ngrad, g1_ref[...], unit, inv)
        gp_ref[r, :] = result

    @pl.loop(0, images)
    def _(i):
        rg_copy(i).wait_send()

    close_up(gp_ref, images)
    grad_save = local_copy(gp_ref.at[flat_rows, :], grad_hbm, save_sem.at[0])
    grad_save.start()
    small_ref[14:18, :] = dwr_ref[0:4, :]

    def small_copy(d):
        return remote(
            small_ref,
            smalls_hbm.at[dp],
            sms_sem.at[d],
            smr_sem.at[d],
            {"dp": lax.rem(dp + d, n_dp)},
        )

    small_own = local_copy(small_ref, smalls_hbm.at[dp], sms_sem.at[0])
    small_own.start()

    @pl.loop(1, n_dp)
    def _(d):
        small_copy(d).start()

    def over_images(left_of, right_of):
        return sum(dot_tn(left_of(b), right_of(b)) for b in range(images // 2))

    def normed_of(c):
        cols = pl.ds(pl.multiple_of(256 + c * 256, 256), 256)
        return lambda b: win_ref[b, pl.ds(0, 416), cols]

    def qk_of(k):
        return lambda b: wout_ref[b // 2, pl.ds((b % 2) * 416, 416), pl.ds(k * 256, 256)]

    def query_key(c, dst):
        dst[:, 0:256] = over_images(normed_of(c), qk_of(0))
        dst[:, 256:512] = over_images(normed_of(c), qk_of(1))

    def value_out(c, dst):
        dst[:, 0:256] = over_images(normed_of(c), lambda b: win_ref[b, pl.ds(0, 416), pl.ds(0, 256)])
        dst[:, 256:512] = over_images(
            lambda b: win_ref[b, pl.ds(0, 416), pl.ds(768, 256)],
            lambda b: og_ref[pl.ds(b * 416, 416), rows(c, 256)],
        )

    for n, fill in ((16, query_key), (17, value_out)):
        exchange_sib(n - 2).wait_send()
        fill(1 - core, sib_ref.at[n % 2])
        exchange_sib(n).start()
        fill(core, acc_ref.at[n % held])
        absorb(n)
        if n == 16:
            service(16, "ABC")
            service(17, "ABC")

    @pl.loop(0, images)
    def _(i):
        r = rows(i, PAD)
        service(18 + i, "ABC")
        comb_copy(i).wait_recv()
        fetch = [
            local_copy(mid_hbm.at[r, :], bufa_ref, img_sem.at[0]),
            local_copy(combl_hbm.at[r, :], bufb_ref, img_sem.at[1]),
        ]
        for copy in fetch:
            copy.start()
        comb_copy(i).wait_send()
        for copy in fetch:
            copy.wait()
        result = bufa_ref[...] + (comb_ref[r, :] + bufb_ref[...])
        comb_ref[r, :] = result

    close_up(comb_ref, images)
    layer_save = local_copy(comb_ref.at[flat_rows, :], layer_hbm, save_sem.at[1])
    layer_save.start()

    smallsum_ref[...] = jnp.zeros_like(smallsum_ref)
    small_own.wait()

    @pl.loop(1, n_dp)
    def _(d):
        source = lax.rem(dp + n_dp - d, n_dp)
        remote(small_ref, smalls_hbm.at[source], sms_sem.at[d], smr_sem.at[d], sibling).wait_recv()

    @pl.loop(0, n_dp // 16)
    def _(g):
        copy = local_copy(smalls_hbm.at[rows(g, 16)], sm_ref, img_sem.at[2])
        copy.start()
        copy.wait()

        @pl.loop(0, 16)
        def _(d):
            smallsum_ref[...] += sm_ref[d]

    @pl.loop(18 + images, FIRST_ATT + 3 + 2 * nz + 2)
    def _(s):
        service(s, "ABC")

    @pl.loop(1, n_dp)
    def _(d):
        small_copy(d).wait_send()

    for n in (16, 17):
        exchange_sib(n).wait_send()

    grad_save.wait()
    layer_save.wait()


def finish_kernel(
    units_hbm,
    layer_in,
    grad_in,
    small_ref,
    layer_out,
    grad_out,
    g1_ref,
    b1_ref,
    dwqkv_hbm,
    qvb_ref,
    dwo_hbm,
    ob_ref,
    g2_ref,
    b2_ref,
    dwr_ref,
    dwin_hbm,
    dib_ref,
    dwout_hbm,
    sem,
    *stages,
):
    pairs = []
    for e in range(4):
        for f in range(2):
            chunk = pl.ds(f * 512, 512)
            pairs.append((units_hbm.at[2 * e + f], dwout_hbm.at[e, chunk, :]))
            pairs.append((units_hbm.at[8 + 2 * e + f], dwin_hbm.at[e, :, chunk]))
    low, high = pl.ds(0, 256), pl.ds(256, 256)
    pairs += [
        (units_hbm.at[16, :, low], dwqkv_hbm.at[0]),
        (units_hbm.at[16, :, high], dwqkv_hbm.at[1]),
        (units_hbm.at[17, :, low], dwqkv_hbm.at[2]),
        (units_hbm.at[17, low, high], dwo_hbm.at[:, low]),
        (units_hbm.at[17, high, high], dwo_hbm.at[:, high]),
        (layer_in, layer_out),
        (grad_in, grad_out),
    ]
    ins = [
        pltpu.make_async_copy(src, stages[k], sem.at[0, k]) for k, (src, _) in enumerate(pairs)
    ]
    results = [
        pltpu.make_async_copy(stages[k], dst, sem.at[1, k]) for k, (_, dst) in enumerate(pairs)
    ]
    for copy in ins:
        copy.start()
    g1_ref[...] = small_ref[0:1, :]
    b1_ref[...] = small_ref[1:2, :]
    g2_ref[...] = small_ref[2:3, :]
    b2_ref[...] = small_ref[3:4, :]
    ob_ref[...] = small_ref[4:5, :]
    qvb_ref[0:1, :] = small_ref[5:6, 0:256]
    qvb_ref[1:2, :] = small_ref[5:6, 256:512]
    for e in range(4):
        for f in range(2):
            k = 6 + 2 * e + f
            dib_ref[e : e + 1, pl.ds(f * 512, 512)] = small_ref[k : k + 1, :]
    dwr_ref[...] = small_ref[14:18, :]
    for copy_in, copy_out in zip(ins, results):
        copy_in.wait()
        copy_out.start()
    for copy in results:
        copy.wait()


def local(
    layer_input,
    cotangent,
    ln1_gain,
    ln1_shift,
    w_qkv,
    qv_bias,
    w_out,
    out_bias,
    ln2_gain,
    ln2_shift,
    w_router,
    w_in,
    in_bias,
    w_hidden_out,
    choices,
    priority,
    *,
    n_dp,
):
    tokens, width = layer_input.shape
    experts = w_in.shape[0]
    capacity = (5 * tokens + 2 * experts - 1) // (2 * experts)
    images = tokens // SEQ
    total = images * PAD
    sds = jax.ShapeDtypeStruct
    vmem = pl.BlockSpec(memory_space=pltpu.VMEM)
    hbm = pl.BlockSpec(memory_space=pl.ANY)
    row = lambda v: v.reshape(1, -1)
    dma = pltpu.SemaphoreType.DMA
    block = (128, width)
    outs = pl.pallas_call(
        functools.partial(main_kernel, n_dp, images, capacity),
        out_shape=(
            sds((UNITS, 512, 512), F32),
            sds((tokens, width), F32),
            sds((tokens, width), F32),
            sds((SMALL, width), F32),
            sds((total, width), F32),
            sds((total, width), F32),
            sds((3, total, width), BF),
            sds((total, width), BF),
            sds((total, 256), BF),
            sds((total, width), F32),
            sds((total, width), F32),
            sds((n_dp, SMALL, width), F32),
        ),
        in_specs=[hbm, hbm] + [vmem] * 11 + [hbm, vmem, hbm],
        out_specs=(hbm, hbm, hbm, vmem) + (hbm,) * 8,
        scratch_shapes=[
            pltpu.VMEM((total, width), BF),
            pltpu.VMEM((total, width), F32),
            pltpu.VMEM((total, LANES), F32),
            pltpu.VMEM(w_in.shape, BF),
            pltpu.VMEM(w_hidden_out.shape, BF),
            pltpu.VMEM((total, width), BF),
            pltpu.VMEM((total, width), BF),
            pltpu.VMEM((experts, total, 1024), BF),
            pltpu.VMEM((total, width), F32),
            pltpu.VMEM((total, width), F32),
            pltpu.VMEM((total, LANES), F32),
            pltpu.VMEM((12 if n_dp <= 16 else UNITS, 256, width), F32),
            pltpu.VMEM((2, 256, width), F32),
            pltpu.VMEM((2, 256, width), F32),
            pltpu.VMEM((4,) + block, F32),
            pltpu.VMEM((SLOTS,) + block, F32),
            pltpu.VMEM((SLOTS,) + block, F32),
            pltpu.VMEM((FINALS if n_dp <= 16 else 1, 256, width), F32),
            pltpu.VMEM((8, total), F32),
            pltpu.VMEM((8, total), F32),
            pltpu.VMEM((SMALL, width), F32),
            pltpu.VMEM((16, SMALL, width), F32),
            pltpu.VMEM((LANES, width), F32),
            pltpu.VMEM(w_qkv.shape, BF),
            pltpu.VMEM(w_out.shape, BF),
            pltpu.VMEM(qv_bias.shape, F32),
            pltpu.VMEM((2, 3, PAD, width), BF),
            pltpu.VMEM((PAD, width), F32),
            pltpu.VMEM((PAD, width), F32),
            pltpu.VMEM((PAD, width), F32),
            dma((9,)),
            dma((7,)),
            dma((2, 2)),
            dma((2, 2)),
            dma((2, 4)),
            dma((2,)),
            dma((2, 3)),
            dma((5,)),
            dma((images,)),
            dma((images,)),
            dma((images,)),
            dma((images,)),
            dma((2,)),
            dma((2,)),
            dma((2,)),
        ]
        + [dma((ENTRIES,)) for _ in range(14)]
        + [dma((UNITS,)), dma((UNITS,)), dma((UNITS,)), dma((ENTRIES,))]
        + [
            dma((n_dp,)),
            dma((n_dp,)),
            pltpu.SemaphoreType.REGULAR,
            pltpu.SemaphoreType.REGULAR,
        ],
        compiler_params=pltpu.CompilerParams(
            collective_id=1, has_side_effects=True, vmem_limit_bytes=63 * MIB
        ),
        name="layer",
    )(
        layer_input,
        cotangent,
        choices.T,
        priority,
        row(ln1_gain),
        row(ln1_shift),
        w_qkv,
        qv_bias,
        w_out,
        row(out_bias),
        row(ln2_gain),
        row(ln2_shift),
        w_router.T,
        w_in,
        in_bias,
        w_hidden_out,
    )
    units, layer_out, input_grad, small = outs[:4]
    vector = sds((1, width), F32)
    results = pl.pallas_call(
        finish_kernel,
        out_shape=(
            sds(layer_input.shape, F32),
            sds(layer_input.shape, F32),
            vector,
            vector,
            sds(w_qkv.shape, F32),
            sds(qv_bias.shape, F32),
            sds(w_out.shape, F32),
            vector,
            vector,
            vector,
            sds(w_router.shape[::-1], F32),
            sds(w_in.shape, F32),
            sds(in_bias.shape, F32),
            sds(w_hidden_out.shape, F32),
        ),
        in_specs=[hbm, hbm, hbm, vmem],
        out_specs=(hbm, hbm, vmem, vmem, hbm, vmem, hbm, vmem, vmem, vmem, vmem, hbm, vmem, hbm),
        scratch_shapes=[dma((2, 23))]
        + [pltpu.VMEM((512, 512), F32)] * 16
        + [pltpu.VMEM((512, 256), F32)] * 3
        + [pltpu.VMEM((256, 256), F32)] * 2
        + [pltpu.VMEM((tokens, width), F32)] * 2,
        compiler_params=pltpu.CompilerParams(vmem_limit_bytes=62 * MIB),
        name="finish",
    )(units, layer_out, input_grad, small)
    results = [v.reshape(width) if v.shape == (1, width) else v for v in results]
    results[10] = results[10].T
    return tuple(results)


def solution(mesh):
    whole = P()
    placed = (
        P("dp", None),
        P("dp", None),
        whole,
        whole,
        P(None, None, "tensor"),
        P(None, "tensor"),
        P("tensor", None),
        whole,
        whole,
        whole,
        whole,
        P(None, None, "tensor"),
        P(None, "tensor"),
        P(None, "tensor", None),
        P("dp", None),
        P("dp", None),
    )
    grads = placed[2:14]
    return jax.shard_map(
        functools.partial(local, n_dp=mesh.shape["dp"]),
        mesh=mesh,
        in_specs=placed,
        out_specs=(P("dp", None), P("dp", None)) + grads,
        check_vma=False,
    )
```
